32 devices in a mesh: hb: 4 (over x, core), wb: 2 (over y), hd: 4 (over z).
Axes of the slice: x: 2, y: 2, z: 4, core: 2. Of those that a mesh axis runs over, the one named last changes fastest.
Arguments:
- query_rows: bfloat16 [12, 4, 4, 64, 128], P('hd', 'hb', 'wb'), may hold values from -180 to 180
- key_rows: bfloat16 [12, 4, 4, 64, 128], P('hd', 'hb', 'wb'), may hold values from -6 to 6
- value_rows: bfloat16 [12, 4, 4, 64, 128], P('hd', 'hb', 'wb'), may hold values from -6 to 6
- grad_out: bfloat16 [12, 4, 4, 64, 128], P('hd', 'hb', 'wb'), may hold values from -6 to 6
- sel_tiles: int32 [4, 4, 8], P(None, 'wb'), may hold values from 0 to 7
- sel_count: int32 [4, 4], P(None, 'wb'), may hold values from 1 to 8, as said below
- tile_radius: int32 [12], P('hd'), may hold values from 0 to 1
Outputs:
- grad_query: bfloat16 [12, 4, 4, 64, 128], P('hd', 'hb', 'wb')
- grad_key: bfloat16 [12, 4, 4, 64, 128], P('hd', 'hb', 'wb')
- grad_value: bfloat16 [12, 4, 4, 64, 128], P('hd', 'hb', 'wb')
The draws below stay inside these ranges and needn't reach their ends.
Inputs may be any that keep to these rules, and one draw needn't show every extreme that they name: sel_count[r, c] is the number of live entries of that query tile's list, from 1 to 8; entries of sel_tiles at positions sel_count or beyond are ignored, and entries may repeat.
All inputs are finite; a program needn't handle non-finite values.
Results may differ from the reference program's by a relative error of at most 0.022.
Values may be sent and summed in bfloat16 or wider, within the bound.
A program may use at most 64 MiB of HBM per device.

```python
import jax
import jax.numpy as jnp
from jax import lax

HD = 128
TILE = 64
SEL = 8
TR = 1
TC = 2
HEADS = 12
GR = 4
GC = 4
N_HB = 4
N_WB = 2


def key_base(key):
    shape = (HEADS, GR, GC, TILE, HD)
    return jax.random.truncated_normal(jax.random.fold_in(key, 7), -6.0, 6.0, shape, jnp.float32)


def draw_key_rows(key, part):
    base = key_base(key)
    return base.astype(jnp.bfloat16)


def draw_query_rows(key, part):
    shape = (HEADS, GR, GC, TILE, HD)
    fresh = jax.random.truncated_normal(jax.random.fold_in(key, 13), -6.0, 6.0, shape, jnp.float32)
    return fresh.astype(jnp.bfloat16)


def draw_sel_count(key, part):
    level = jax.random.randint(jax.random.fold_in(key, 29), (GR, 1), 1, 5)
    base = jax.random.randint(jax.random.fold_in(key, 31), (GR, GC), 0, SEL)
    counted = 1 + base * level // 4
    pick_row = jax.random.randint(jax.random.fold_in(key, 37), (), 0, GR)
    pick_col = jax.random.randint(jax.random.fold_in(key, 41), (), 0, GC)
    marked = (jnp.arange(GR)[:, None] == pick_row) & (jnp.arange(GC)[None, :] == pick_col)
    return jnp.where(marked, SEL, counted).astype(jnp.int32)


def draw_tile_radius(key, part):
    picked = jax.random.randint(jax.random.fold_in(key, 23), (HEADS,), 0, 2)
    order = jax.random.permutation(jax.random.fold_in(key, 43), HEADS)
    picked = picked.at[order[0]].set(0)
    picked = picked.at[order[1]].set(1)
    return picked.astype(jnp.int32)


def touch_ends(entries, own_key, smallest, top_value):
    index_at = [jax.random.randint(jax.random.fold_in(own_key, axis), (), 0, length) for axis, length in enumerate(entries.shape)]
    widest = entries.shape.index(max(entries.shape))
    beside = index_at[:widest] + [(index_at[widest] + 1) % entries.shape[widest]] + index_at[widest + 1:]
    return entries.at[tuple(index_at)].set(smallest).at[tuple(beside)].set(top_value)


def levels(own_key, extent, pieces, low, top_value):
    gain = 1.0
    for axis_at, shards_of in pieces:
        steps = jax.random.uniform(jax.random.fold_in(jax.random.fold_in(own_key, 6), axis_at), (shards_of,), jnp.float32, low / len(pieces), top_value / len(pieces))
        gain = gain * jnp.repeat(jnp.exp(steps), extent[axis_at] // shards_of).reshape((-1,) + (1,) * (len(extent) - 1 - axis_at))
    return gain


def normal_values(key, dims, scale, bound, pieces=(), kind=jnp.bfloat16):
    entries = scale * jax.random.normal(key, dims, jnp.float32)
    if pieces:
        entries = entries * levels(key, dims, pieces, -0.22, 0.18)
    return jnp.clip(entries, -bound, bound).astype(kind)


def setup_inputs(seed: int = 0) -> dict:
    key_list = jax.random.split(jax.random.key(seed), 8)
    return {
        "query_rows": draw_query_rows(jax.random.fold_in(key_list[7], 71), 0),
        "key_rows": draw_key_rows(jax.random.fold_in(key_list[7], 71), 0),
        "value_rows": normal_values(key_list[2], (HEADS, GR, GC, TILE, HD), 1.0, 6.0, ((0, 4), (1, 4), (2, 2))),
        "grad_out": normal_values(key_list[3], (HEADS, GR, GC, TILE, HD), 1.0, 6.0, ((0, 4), (1, 4), (2, 2))),
        "sel_tiles": touch_ends(jax.random.randint(key_list[4], (GR, GC, SEL), 0, GR * TC), jax.random.fold_in(key_list[4], 1), 0, (GR * TC) - 1).astype(jnp.int32),
        "sel_count": draw_sel_count(jax.random.fold_in(key_list[7], 71), 0),
        "tile_radius": draw_tile_radius(jax.random.fold_in(key_list[7], 71), 0),
    }


def settle(values):
    return lax.optimization_barrier(values.astype(jnp.bfloat16)).astype(jnp.float32)


def tile_masks(tile_radius, sel_tiles, sel_count):
    band_rows, band_cols, picks = sel_tiles.shape
    tile_total = band_rows * band_cols
    tile_index = jnp.arange(tile_total, dtype=jnp.int32)
    row_of = tile_index // band_cols
    col_of = tile_index % band_cols
    spread = jnp.abs(row_of[:, None] - row_of[None, :]) + jnp.abs(col_of[:, None] - col_of[None, :])
    nearby = spread[None] <= tile_radius[:, None, None]
    live_pick = jnp.arange(picks, dtype=jnp.int32)[None, :] < sel_count.reshape(tile_total, 1)
    matches = (sel_tiles.reshape(tile_total, picks, 1) == tile_index[None, None, :]) & live_pick[:, :, None]
    return nearby | jnp.any(matches, axis=1)[None]


def to_band(values):
    extra = values.shape[3:]
    moved = jnp.moveaxis(values.reshape((GR, N_WB, TC, TILE) + extra), 1, 0)
    return moved.reshape((N_WB, GR * TC * TILE) + extra)


def to_grid(values):
    extra = values.shape[2:]
    moved = jnp.moveaxis(values.reshape((N_WB, GR, TC, TILE) + extra), 0, 1)
    return moved.reshape((GR, GC, TILE) + extra)


def head_grads(query, keyrow, valrow, cotan, radius, allowed):
    factor = HD ** -0.5
    f32 = jnp.float32
    query_f = query.astype(f32)
    key_f = keyrow.astype(f32)
    value_f = valrow.astype(f32)
    cotan_f = cotan.astype(f32)
    band_q = to_band(query_f)
    band_k = to_band(key_f)
    band_v = to_band(value_f)
    band_d = to_band(cotan_f)
    tile_total = GR * TC
    band_scores = jnp.einsum("nqd,nkd->nqk", band_q, band_k) * factor
    shaped = band_scores.reshape(N_WB, tile_total, TILE, tile_total, TILE)
    band_scores = jnp.where(allowed[:, :, None, :, None], shaped, -jnp.inf).reshape(N_WB, tile_total * TILE, tile_total * TILE)
    zero_col = jnp.zeros_like(key_f[:, :1])
    left_keys = jnp.concatenate([zero_col, key_f[:, :-1]], axis=1)
    right_keys = jnp.concatenate([key_f[:, 1:], zero_col], axis=1)
    left_vals = jnp.concatenate([zero_col, value_f[:, :-1]], axis=1)
    right_vals = jnp.concatenate([value_f[:, 1:], zero_col], axis=1)
    column = jnp.arange(GC, dtype=jnp.int32)
    left_ok = (column % TC == 0) & (column >= 1) & (radius >= 1)
    right_ok = (column % TC == TC - 1) & (column <= GC - 2) & (radius >= 1)
    left_scores = jnp.einsum("rcid,rcjd->rcij", query_f, left_keys) * factor
    left_scores = jnp.where(left_ok[None, :, None, None], left_scores, -jnp.inf)
    right_scores = jnp.einsum("rcid,rcjd->rcij", query_f, right_keys) * factor
    right_scores = jnp.where(right_ok[None, :, None, None], right_scores, -jnp.inf)
    top = to_grid(jnp.max(band_scores, axis=-1))
    top = jnp.maximum(top, jnp.max(left_scores, axis=-1))
    top = jnp.maximum(top, jnp.max(right_scores, axis=-1))
    total = to_grid(jnp.sum(jnp.exp(band_scores - to_band(top)[..., None]), axis=-1))
    total = total + jnp.sum(jnp.exp(left_scores - top[..., None]), axis=-1)
    total = total + jnp.sum(jnp.exp(right_scores - top[..., None]), axis=-1)
    log_sum = top + jnp.log(total)
    band_probs = jnp.exp(band_scores - to_band(log_sum)[..., None])
    left_probs = jnp.exp(left_scores - log_sum[..., None])
    right_probs = jnp.exp(right_scores - log_sum[..., None])
    band_half = settle(band_probs)
    left_half = settle(left_probs)
    right_half = settle(right_probs)
    output = to_grid(jnp.einsum("nqk,nkd->nqd", band_half, band_v))
    output = output + jnp.einsum("rcij,rcjd->rcid", left_half, left_vals)
    output = output + jnp.einsum("rcij,rcjd->rcid", right_half, right_vals)
    delta = jnp.sum(cotan_f * output, axis=-1)
    band_slopes = jnp.einsum("nqd,nkd->nqk", band_d, band_v)
    band_grad = settle(band_probs * (band_slopes - to_band(delta)[..., None]) * factor)
    left_slopes = jnp.einsum("rcid,rcjd->rcij", cotan_f, left_vals)
    left_grad = settle(left_probs * (left_slopes - delta[..., None]) * factor)
    right_slopes = jnp.einsum("rcid,rcjd->rcij", cotan_f, right_vals)
    right_grad = settle(right_probs * (right_slopes - delta[..., None]) * factor)
    grad_q = to_grid(jnp.einsum("nqk,nkd->nqd", band_grad, band_k))
    grad_q = grad_q + jnp.einsum("rcij,rcjd->rcid", left_grad, left_keys)
    grad_q = grad_q + jnp.einsum("rcij,rcjd->rcid", right_grad, right_keys)
    dev_rows = TR * TC * TILE
    grad_groups = band_grad.reshape(N_WB, N_HB, dev_rows, tile_total * TILE)
    half_groups = band_half.reshape(N_WB, N_HB, dev_rows, tile_total * TILE)
    query_groups = band_q.reshape(N_WB, N_HB, dev_rows, HD)
    cotan_groups = band_d.reshape(N_WB, N_HB, dev_rows, HD)
    key_band = jnp.sum(settle(jnp.einsum("ngqk,ngqd->ngkd", grad_groups, query_groups)), axis=1)
    value_band = jnp.sum(settle(jnp.einsum("ngqk,ngqd->ngkd", half_groups, cotan_groups)), axis=1)
    zero_grid = jnp.zeros_like(query_f[:, :1])
    left_key = jnp.einsum("rcij,rcid->rcjd", left_grad, query_f)
    right_key = jnp.einsum("rcij,rcid->rcjd", right_grad, query_f)
    left_value = jnp.einsum("rcij,rcid->rcjd", left_half, cotan_f)
    right_value = jnp.einsum("rcij,rcid->rcjd", right_half, cotan_f)
    grad_k = to_grid(key_band) + jnp.concatenate([left_key[:, 1:], zero_grid], axis=1) + jnp.concatenate([zero_grid, right_key[:, :-1]], axis=1)
    grad_v = to_grid(value_band) + jnp.concatenate([left_value[:, 1:], zero_grid], axis=1) + jnp.concatenate([zero_grid, right_value[:, :-1]], axis=1)
    return grad_q.astype(jnp.bfloat16), grad_k.astype(jnp.bfloat16), grad_v.astype(jnp.bfloat16)


def reference(query_rows, key_rows, value_rows, grad_out, sel_tiles, sel_count, tile_radius):
    band_sel = jnp.moveaxis(sel_tiles.reshape(GR, N_WB, TC, SEL), 1, 0)
    band_count = jnp.moveaxis(sel_count.reshape(GR, N_WB, TC), 1, 0)

    def band_mask(picked, counted):
        return tile_masks(tile_radius, picked, counted)

    allowed = jnp.moveaxis(jax.vmap(band_mask)(band_sel, band_count), 1, 0)

    def per_head(items):
        return head_grads(items[0], items[1], items[2], items[3], items[4], items[5])

    grad_query, grad_key, grad_value = lax.map(per_head, (query_rows, key_rows, value_rows, grad_out, tile_radius, allowed))
    return grad_query, grad_key, grad_value
```

```python
import functools

import jax
import jax.numpy as jnp
from jax import lax
from jax.experimental import pallas as pl
from jax.experimental.pallas import tpu as pltpu
from jax.sharding import PartitionSpec as P

MESH = pl.DeviceIdType.MESH
F32 = jnp.float32
BF16 = jnp.bfloat16
NT = (((1,), (1,)), ((), ()))
NN = (((1,), (0,)), ((), ()))
TN = (((0,), (0,)), ((), ()))


def dot(a, b, dims):
    return lax.dot_general(a, b, dims, preferred_element_type=F32)


def kernel(
    dims,
    q_hbm, k_hbm, v_hbm, g_hbm, sel_ref, count_ref, radius_ref,
    dq_ref, dk_ref, dv_ref,
    qg, kv, acc_own, acc_chip, tx_sib, rx_sib, tx_chip, rx_chip, tx_edge, rx_edge,
    q_sem, kv_sem, s_kvsib, r_kvsib, s_kvchip, r_kvchip, s_relay, r_relay, s_kvedge, r_kvedge,
    s_psib, r_psib, s_pchip, r_pchip, s_pedge, r_pedge,
):
    heads, trows, tcols, tile, picks, n_hb, n_wb, factor = dims
    rows = trows * tcols * tile
    chips = n_hb // 2
    me = lax.axis_index("hb")
    w = lax.axis_index("wb")
    chip, core = me // 2, me % 2
    sib = chip * 2 + 1 - core
    to_chip = {j: ((chip + j) % chips) * 2 + core for j in range(1, chips)}
    from_chip = {j: ((chip + chips - j) % chips) * 2 + core for j in range(1, chips)}
    if n_wb == 1:
        links = []
    elif n_wb == 2:
        links = [(None, 1 - w, 0, 0, (1 - w) * (tcols - 1))]
    else:
        links = [(w > 0, w - 1, 0, 1, 0), (w < n_wb - 1, w + 1, 1, 0, tcols - 1)]

    def guarded(there, fn):
        if there is None:
            fn()
        else:
            pl.when(there)(fn)

    def remote(src, dst, send, recv, axis, to):
        return pltpu.make_async_remote_copy(
            src_ref=src, dst_ref=dst, send_sem=send, recv_sem=recv,
            device_id={axis: to}, device_id_type=MESH,
        )

    own_kv = []
    for h in range(heads):
        own_kv.append((
            pltpu.make_async_copy(k_hbm.at[h], kv.at[0, h, pl.ds(0, rows)], kv_sem.at[h, 0]),
            pltpu.make_async_copy(v_hbm.at[h], kv.at[1, h, pl.ds(0, rows)], kv_sem.at[h, 1]),
        ))
        for c in own_kv[-1]:
            c.start()
    own_q = [
        pltpu.make_async_copy(q_hbm, qg.at[0], q_sem.at[0]),
        pltpu.make_async_copy(g_hbm, qg.at[1], q_sem.at[1]),
    ]
    for c in own_q:
        c.start()

    barrier = pltpu.get_barrier_semaphore()
    pl.semaphore_signal(barrier, inc=1, device_id={"hb": sib}, device_id_type=MESH)
    for j in range(1, chips):
        pl.semaphore_signal(barrier, inc=1, device_id={"hb": to_chip[j]}, device_id_type=MESH)
    for there, peer, _, _, _ in links:
        def hello(peer=peer):
            pl.semaphore_signal(barrier, inc=1, device_id={"wb": peer}, device_id_type=MESH)
        guarded(there, hello)
    if n_wb > 2:
        for slot, (there, _, _, _, _) in enumerate(links):
            def blank(slot=slot):
                at = n_hb * rows + slot * trows * tile
                kv[:, :, pl.ds(at, trows * tile), :] = jnp.zeros(
                    (2, heads, trows * tile, kv.shape[-1]), BF16)
            pl.when(jnp.logical_not(there))(blank)
    greeted = chips
    for there, _, _, _, _ in links:
        greeted = greeted + (1 if there is None else jnp.where(there, 1, 0))
    pl.semaphore_wait(barrier, greeted)

    def slot_at(s):
        return pl.ds(s * rows, rows)

    def edge_at(slot, r):
        return pl.ds(n_hb * rows + (slot * trows + r) * tile, tile)

    def kv_chip(h, j):
        return remote(kv.at[:, h, slot_at(0)], kv.at[:, h, slot_at(2 * j)],
                      s_kvchip.at[h, j], r_kvchip.at[h, j], "hb", to_chip[j])

    def kv_sib(h):
        return remote(kv.at[:, h, slot_at(0)], kv.at[:, h, slot_at(1)],
                      s_kvsib.at[h], r_kvsib.at[h], "hb", sib)

    def relay(h, j):
        return remote(kv.at[:, h, slot_at(2 * j)], kv.at[:, h, slot_at(2 * j + 1)],
                      s_relay.at[h, j], r_relay.at[h, j], "hb", sib)

    def own_tile(r, col):
        return pl.ds(pl.multiple_of((r * tcols + col) * tile, tile), tile)

    def kv_edge(h, link, r, arriving=False):
        _, peer, here, away, col = link
        slot = here if arriving else away
        return remote(kv.at[:, h, own_tile(r, col)], kv.at[:, h, edge_at(slot, r)],
                      s_kvedge.at[h, away, r], r_kvedge.at[h, slot, r], "wb", peer)

    def p_sib(h, j):
        return remote(tx_sib.at[h, j], rx_sib.at[h, j], s_psib.at[h, j], r_psib.at[h, j], "hb", sib)

    def p_chip(h, j):
        return remote(tx_chip.at[h, j], rx_chip.at[h, j],
                      s_pchip.at[h, j], r_pchip.at[h, j], "hb", from_chip[j])

    def p_edge(h, link, arriving=False):
        _, peer, here, away, _ = link
        slot = here if arriving else away
        return remote(tx_edge.at[h, here], rx_edge.at[h, slot],
                      s_pedge.at[h, here], r_pedge.at[h, slot], "wb", peer)

    for h in range(heads):
        for c in own_kv[h]:
            c.wait()
        for j in range(1, chips):
            kv_chip(h, j).start()
        kv_sib(h).start()
        for link in links:
            def send(link=link, h=h):
                for r in range(trows):
                    kv_edge(h, link, r).start()
            guarded(link[0], send)

    lane_tile = lax.broadcasted_iota(jnp.int32, (1, rows), 1) // tile
    lane_row = me * trows + lane_tile // tcols
    lane_col = lane_tile % tcols
    chosen = []
    for s in range(picks):
        entry = jnp.full((1, rows), -1, jnp.int32)
        for r in range(trows):
            for c in range(tcols):
                row = me * trows + r
                value = jnp.where(s < count_ref[row, c], sel_ref[row, c, s], -1)
                entry = jnp.where(lane_tile == r * tcols + c, value, entry)
        chosen.append(entry)
    spread, picked = [], []
    for s in range(n_hb):
        j = s // 2
        group = ((chip + chips - j) % chips) * 2 + (core if s % 2 == 0 else 1 - core)
        for r in range(trows):
            for c in range(tcols):
                key_row = group * trows + r
                spread.append(jnp.abs(lane_row - key_row) + jnp.abs(lane_col - c))
                at = key_row * tcols + c
                hit = functools.reduce(jnp.logical_or, [e == at for e in chosen])
                picked.append(hit)
    beside = []
    for there, _, slot, _, col in links:
        for r in range(trows):
            near = lane_tile == r * tcols + col
            if there is not None:
                near = jnp.logical_and(near, there)
            beside.append(near)

    for c in own_q:
        c.wait()

    def compute(h):
        q = qg[0, h]
        g = qg[1, h]
        keys = kv[0, h]
        vals = kv[1, h]
        radius = radius_ref[h]
        bias = [jnp.where(jnp.logical_or(sp <= radius, pk), 0.0, -jnp.inf)
                for sp, pk in zip(spread, picked)]
        bias += [jnp.where(jnp.logical_and(near, radius >= 1), 0.0, -jnp.inf) for near in beside]
        scores = dot(keys, q, NT)
        slopes = dot(vals, g, NT)
        s_t = [scores[i * tile:(i + 1) * tile] * factor + b for i, b in enumerate(bias)]
        d_t = [slopes[i * tile:(i + 1) * tile] for i in range(len(bias))]
        top = jnp.max(functools.reduce(jnp.maximum, s_t), axis=0, keepdims=True)
        e_t = [jnp.exp(s - top) for s in s_t]
        total = jnp.sum(functools.reduce(jnp.add, e_t), axis=0, keepdims=True)
        mixed = jnp.sum(functools.reduce(jnp.add, [e * d for e, d in zip(e_t, d_t)]),
                        axis=0, keepdims=True)
        inverse = 1.0 / total
        delta = mixed * inverse
        probs = [e * inverse for e in e_t]
        half = jnp.concatenate([p.astype(BF16) for p in probs], axis=0)
        grad = jnp.concatenate(
            [(p * ((d - delta) * factor)).astype(BF16) for p, d in zip(probs, d_t)], axis=0)
        return q, g, keys, half, grad

    for h in range(heads):
        for j in range(1, chips):
            kv_chip(h, j).wait_recv()
            relay(h, j).start()
        kv_sib(h).wait_recv()
        for link in links:
            def arrive(link=link, h=h):
                for r in range(trows):
                    kv_edge(h, link, r, True).wait_recv()
            guarded(link[0], arrive)
        for j in range(1, chips):
            relay(h, j).wait_recv()
        q, g, keys, half, grad = compute(h)
        if chips > 1:
            far = slice(2 * rows, n_hb * rows)
            far_parts = (dot(grad[far], q, NN), dot(half[far], g, NN))
            for j in range(1, chips):
                at = (2 * j - 2) * rows
                for i, part in enumerate(far_parts):
                    tx_sib[h, j, i] = part[at + rows:at + 2 * rows].astype(BF16)
                    acc_chip[h, j, i] = part[at:at + rows]
                p_sib(h, j).start()
        near_parts = (dot(grad[:2 * rows], q, NN), dot(half[:2 * rows], g, NN))
        for i, part in enumerate(near_parts):
            tx_sib[h, 0, i] = part[rows:].astype(BF16)
            acc_own[h, i] = part[:rows]
        p_sib(h, 0).start()
        if links:
            edge_parts = (dot(grad[n_hb * rows:], q, NN), dot(half[n_hb * rows:], g, NN))
            for link in links:
                here = link[2]
                for i, part in enumerate(edge_parts):
                    tx_edge[h, here, i] = part[here * trows * tile:(here + 1) * trows * tile].astype(BF16)
                guarded(link[0], lambda link=link, h=h: p_edge(h, link).start())
        dq_ref[h] = dot(grad, keys, TN).astype(BF16)
        for j in range(1, chips):
            p_sib(h, j).wait_recv()
            for i in range(2):
                tx_chip[h, j, i] = (acc_chip[h, j, i] + rx_sib[h, j, i].astype(F32)).astype(BF16)
            p_chip(h, j).start()

    for h in range(heads):
        p_sib(h, 0).wait_recv()
        for link in links:
            there, _, here, _, col = link

            def add_edge(link=link, here=here, col=col, h=h):
                p_edge(h, link, True).wait_recv()
                for i in range(2):
                    for r in range(trows):
                        at = own_tile(r, col)
                        acc_own[h, i, at] += rx_edge[h, here, i, pl.ds(r * tile, tile)].astype(F32)
            guarded(there, add_edge)
        totals = [acc_own[h, i] + rx_sib[h, 0, i].astype(F32) for i in range(2)]
        for j in range(1, chips):
            p_chip(h, j).wait_recv()
            for i in range(2):
                totals[i] = totals[i] + rx_chip[h, j, i].astype(F32)
        dk_ref[h] = totals[0].astype(BF16)
        dv_ref[h] = totals[1].astype(BF16)

    for h in range(heads):
        kv_sib(h).wait_send()
        p_sib(h, 0).wait_send()
        for j in range(1, chips):
            kv_chip(h, j).wait_send()
            relay(h, j).wait_send()
            p_sib(h, j).wait_send()
            p_chip(h, j).wait_send()
        for link in links:
            def drain(link=link, h=h):
                for r in range(trows):
                    kv_edge(h, link, r).wait_send()
                p_edge(h, link).wait_send()
            guarded(link[0], drain)


def on_device(n_hb, n_wb, query_rows, key_rows, value_rows, grad_out, sel_tiles, sel_count, tile_radius):
    heads, trows, tcols, tile, depth = query_rows.shape
    picks = sel_tiles.shape[-1]
    rows = trows * tcols * tile
    chips = n_hb // 2
    sides = max(1, min(2, n_wb - 1))
    used = min(2, n_wb - 1)
    flat = (heads, rows, depth)
    keys = n_hb * rows + used * trows * tile
    dma = pltpu.SemaphoreType.DMA
    dims = (heads, trows, tcols, tile, picks, n_hb, n_wb, depth ** -0.5)
    any_spec = pl.BlockSpec(memory_space=pl.ANY)
    smem = pl.BlockSpec(memory_space=pltpu.SMEM)
    vmem = pl.BlockSpec(memory_space=pltpu.VMEM)
    out = jax.ShapeDtypeStruct(flat, BF16)
    results = pl.pallas_call(
        functools.partial(kernel, dims),
        out_shape=(out, out, out),
        in_specs=[any_spec] * 4 + [smem] * 3,
        out_specs=(vmem,) * 3,
        scratch_shapes=[
            pltpu.VMEM((2,) + flat, BF16),
            pltpu.VMEM((2, heads, keys, depth), BF16),
            pltpu.VMEM((heads, 2, rows, depth), F32),
            pltpu.VMEM((heads, chips, 2, rows, depth), F32),
            pltpu.VMEM((heads, chips, 2, rows, depth), BF16),
            pltpu.VMEM((heads, chips, 2, rows, depth), BF16),
            pltpu.VMEM((heads, chips, 2, rows, depth), BF16),
            pltpu.VMEM((heads, chips, 2, rows, depth), BF16),
            pltpu.VMEM((heads, sides, 2, trows * tile, depth), BF16),
            pltpu.VMEM((heads, sides, 2, trows * tile, depth), BF16),
            dma((2,)), dma((heads, 2)),
            dma((heads,)), dma((heads,)),
            dma((heads, chips)), dma((heads, chips)),
            dma((heads, chips)), dma((heads, chips)),
            dma((heads, sides, trows)), dma((heads, sides, trows)),
            dma((heads, chips)), dma((heads, chips)),
            dma((heads, chips)), dma((heads, chips)),
            dma((heads, sides)), dma((heads, sides)),
        ],
        compiler_params=pltpu.CompilerParams(
            collective_id=0, has_side_effects=True, vmem_limit_bytes=48 * 1024 * 1024),
        cost_estimate=pl.CostEstimate(
            flops=10 * heads * rows * keys * depth,
            bytes_accessed=14 * heads * rows * depth,
            transcendentals=heads * rows * keys),
    )(
        query_rows.reshape(flat), key_rows.reshape(flat), value_rows.reshape(flat),
        grad_out.reshape(flat), sel_tiles, sel_count, tile_radius,
    )
    return tuple(r.reshape(query_rows.shape) for r in results)


def solution(mesh):
    block = P("hd", "hb", "wb", None, None)
    return jax.shard_map(
        functools.partial(on_device, mesh.shape["hb"], mesh.shape["wb"]),
        mesh=mesh,
        in_specs=(block, block, block, block, P(None, "wb", None), P(None, "wb"), P("hd")),
        out_specs=(block, block, block),
        check_vma=False,
    )
```

```python
import functools

import jax
import jax.numpy as jnp
from jax import lax
from jax.experimental import pallas as pl
from jax.experimental.pallas import tpu as pltpu
from jax.sharding import PartitionSpec as P

MESH = pl.DeviceIdType.MESH
F32 = jnp.float32
BF16 = jnp.bfloat16
NT = (((1,), (1,)), ((), ()))
NN = (((1,), (0,)), ((), ()))
TN = (((0,), (0,)), ((), ()))


def dot(a, b, dims):
    return lax.dot_general(a, b, dims, preferred_element_type=F32)


def kernel(
    dims,
    q_hbm, k_hbm, v_hbm, g_hbm, sel_ref, count_ref, radius_ref,
    out_ref,
    qg, kv, acc_own, acc_chip, tx_sib, rx_sib, tx_chip, rx_chip, tx_edge, rx_edge,
    q_sem, kv_sem, s_kvsib, r_kvsib, s_kvchip, r_kvchip, s_relay, r_relay, s_kvedge, r_kvedge,
    s_psib, r_psib, s_pchip, r_pchip, s_pedge, r_pedge,
):
    heads, trows, tcols, tile, picks, n_hb, n_wb, factor = dims
    rows = trows * tcols * tile
    chips = n_hb // 2
    me = lax.axis_index("hb")
    w = lax.axis_index("wb")
    chip, core = me // 2, me % 2
    sib = chip * 2 + 1 - core
    to_chip = {j: ((chip + j) % chips) * 2 + core for j in range(1, chips)}
    from_chip = {j: ((chip + chips - j) % chips) * 2 + core for j in range(1, chips)}
    if n_wb == 1:
        links = []
    elif n_wb == 2:
        links = [(None, 1 - w, 0, 0, (1 - w) * (tcols - 1))]
    else:
        links = [(w > 0, w - 1, 0, 1, 0), (w < n_wb - 1, w + 1, 1, 0, tcols - 1)]

    def guarded(there, fn):
        if there is None:
            fn()
        else:
            pl.when(there)(fn)

    def remote(src, dst, send, recv, axis, to):
        return pltpu.make_async_remote_copy(
            src_ref=src, dst_ref=dst, send_sem=send, recv_sem=recv,
            device_id={axis: to}, device_id_type=MESH,
        )

    own_kv = []
    for h in range(heads):
        own_kv.append((
            pltpu.make_async_copy(k_hbm.at[h], kv.at[0, h, pl.ds(0, rows)], kv_sem.at[h, 0]),
            pltpu.make_async_copy(v_hbm.at[h], kv.at[1, h, pl.ds(0, rows)], kv_sem.at[h, 1]),
        ))
        for c in own_kv[-1]:
            c.start()
    own_q = [
        pltpu.make_async_copy(q_hbm, qg.at[0], q_sem.at[0]),
        pltpu.make_async_copy(g_hbm, qg.at[1], q_sem.at[1]),
    ]
    for c in own_q:
        c.start()

    barrier = pltpu.get_barrier_semaphore()
    pl.semaphore_signal(barrier, inc=1, device_id={"hb": sib}, device_id_type=MESH)
    for j in range(1, chips):
        pl.semaphore_signal(barrier, inc=1, device_id={"hb": to_chip[j]}, device_id_type=MESH)
    for there, peer, _, _, _ in links:
        def hello(peer=peer):
            pl.semaphore_signal(barrier, inc=1, device_id={"wb": peer}, device_id_type=MESH)
        guarded(there, hello)
    if n_wb > 2:
        for slot, (there, _, _, _, _) in enumerate(links):
            def blank(slot=slot):
                at = n_hb * rows + slot * trows * tile
                kv[:, :, pl.ds(at, trows * tile), :] = jnp.zeros(
                    (2, heads, trows * tile, kv.shape[-1]), BF16)
            pl.when(jnp.logical_not(there))(blank)
    greeted = chips
    for there, _, _, _, _ in links:
        greeted = greeted + (1 if there is None else jnp.where(there, 1, 0))
    pl.semaphore_wait(barrier, greeted)

    def slot_at(s):
        return pl.ds(s * rows, rows)

    def edge_at(slot, r):
        return pl.ds(n_hb * rows + (slot * trows + r) * tile, tile)

    def kv_chip(h, j):
        return remote(kv.at[:, h, slot_at(0)], kv.at[:, h, slot_at(2 * j)],
                      s_kvchip.at[h, j], r_kvchip.at[h, j], "hb", to_chip[j])

    def kv_sib(h):
        return remote(kv.at[:, h, slot_at(0)], kv.at[:, h, slot_at(1)],
                      s_kvsib.at[h], r_kvsib.at[h], "hb", sib)

    def relay(h, j):
        return remote(kv.at[:, h, slot_at(2 * j)], kv.at[:, h, slot_at(2 * j + 1)],
                      s_relay.at[h, j], r_relay.at[h, j], "hb", sib)

    def own_tile(r, col):
        return pl.ds(pl.multiple_of((r * tcols + col) * tile, tile), tile)

    def kv_edge(h, link, r, arriving=False):
        _, peer, here, away, col = link
        slot = here if arriving else away
        return remote(kv.at[:, h, own_tile(r, col)], kv.at[:, h, edge_at(slot, r)],
                      s_kvedge.at[h, away, r], r_kvedge.at[h, slot, r], "wb", peer)

    def p_sib(h, j):
        return remote(tx_sib.at[h, j], rx_sib.at[h, j], s_psib.at[h, j], r_psib.at[h, j], "hb", sib)

    def p_chip(h, j):
        return remote(tx_chip.at[h, j], rx_chip.at[h, j],
                      s_pchip.at[h, j], r_pchip.at[h, j], "hb", from_chip[j])

    def p_edge(h, link, arriving=False):
        _, peer, here, away, _ = link
        slot = here if arriving else away
        return remote(tx_edge.at[h, here], rx_edge.at[h, slot],
                      s_pedge.at[h, here], r_pedge.at[h, slot], "wb", peer)

    for h in range(heads):
        for c in own_kv[h]:
            c.wait()
        for j in range(1, chips):
            kv_chip(h, j).start()
        kv_sib(h).start()
        for link in links:
            def send(link=link, h=h):
                for r in range(trows):
                    kv_edge(h, link, r).start()
            guarded(link[0], send)

    lane_tile = lax.broadcasted_iota(jnp.int32, (1, rows), 1) // tile
    lane_row = me * trows + lane_tile // tcols
    lane_col = lane_tile % tcols
    chosen = []
    for s in range(picks):
        entry = jnp.full((1, rows), -1, jnp.int32)
        for r in range(trows):
            for c in range(tcols):
                row = me * trows + r
                value = jnp.where(s < count_ref[c, row], sel_ref[row, c, s], -1)
                entry = jnp.where(lane_tile == r * tcols + c, value, entry)
        chosen.append(entry)
    spread, picked = [], []
    for s in range(n_hb):
        j = s // 2
        group = ((chip + chips - j) % chips) * 2 + (core if s % 2 == 0 else 1 - core)
        for r in range(trows):
            for c in range(tcols):
                key_row = group * trows + r
                spread.append(jnp.abs(lane_row - key_row) + jnp.abs(lane_col - c))
                at = key_row * tcols + c
                hit = functools.reduce(jnp.logical_or, [e == at for e in chosen])
                picked.append(hit)
    beside = []
    for there, _, slot, _, col in links:
        for r in range(trows):
            near = lane_tile == r * tcols + col
            if there is not None:
                near = jnp.logical_and(near, there)
            beside.append(near)

    for c in own_q:
        c.wait()

    def compute(h):
        q = qg[0, h]
        g = qg[1, h]
        keys = kv[0, h]
        vals = kv[1, h]
        radius = radius_ref[h]
        bias = [jnp.where(jnp.logical_or(sp <= radius, pk), 0.0, -jnp.inf)
                for sp, pk in zip(spread, picked)]
        bias += [jnp.where(jnp.logical_and(near, radius >= 1), 0.0, -jnp.inf) for near in beside]
        scores = dot(keys, q, NT)
        slopes = dot(vals, g, NT)
        s_t = [scores[i * tile:(i + 1) * tile] * factor + b for i, b in enumerate(bias)]
        d_t = [slopes[i * tile:(i + 1) * tile] for i in range(len(bias))]
        top = jnp.max(functools.reduce(jnp.maximum, s_t), axis=0, keepdims=True)
        e_t = [jnp.exp(s - top) for s in s_t]
        total = jnp.sum(functools.reduce(jnp.add, e_t), axis=0, keepdims=True)
        mixed = jnp.sum(functools.reduce(jnp.add, [e * d for e, d in zip(e_t, d_t)]),
                        axis=0, keepdims=True)
        inverse = 1.0 / total
        delta = mixed * inverse
        probs = [e * inverse for e in e_t]
        half = jnp.concatenate([p.astype(BF16) for p in probs], axis=0)
        grad = jnp.concatenate(
            [(p * ((d - delta) * factor)).astype(BF16) for p, d in zip(probs, d_t)], axis=0)
        return q, g, keys, half, grad

    def pass_on(h):
        for j in range(1, chips):
            kv_chip(h, j).wait_recv()
            relay(h, j).start()

    pass_on(0)
    for h in range(heads):
        kv_sib(h).wait_recv()
        for link in links:
            def arrive(link=link, h=h):
                for r in range(trows):
                    kv_edge(h, link, r, True).wait_recv()
            guarded(link[0], arrive)
        for j in range(1, chips):
            relay(h, j).wait_recv()
        q, g, keys, half, grad = compute(h)
        if chips > 1:
            far = slice(2 * rows, n_hb * rows)
            far_parts = (dot(grad[far], q, NN), dot(half[far], g, NN))
            for j in range(1, chips):
                at = (2 * j - 2) * rows
                for i, part in enumerate(far_parts):
                    tx_sib[h, j, i] = part[at + rows:at + 2 * rows].astype(BF16)
                    acc_chip[h, j, i] = part[at:at + rows]
                p_sib(h, j).start()
        if h + 1 < heads:
            pass_on(h + 1)
        near_parts = (dot(grad[:2 * rows], q, NN), dot(half[:2 * rows], g, NN))
        for i, part in enumerate(near_parts):
            tx_sib[h, 0, i] = part[rows:].astype(BF16)
            acc_own[h, i] = part[:rows]
        p_sib(h, 0).start()
        if links:
            edge_parts = (dot(grad[n_hb * rows:], q, NN), dot(half[n_hb * rows:], g, NN))
            for link in links:
                here = link[2]
                for i, part in enumerate(edge_parts):
                    tx_edge[h, here, i] = part[here * trows * tile:(here + 1) * trows * tile].astype(BF16)
                guarded(link[0], lambda link=link, h=h: p_edge(h, link).start())
        out_ref[0, h] = dot(grad, keys, TN).astype(BF16)
        for j in range(1, chips):
            p_sib(h, j).wait_recv()
            for i in range(2):
                tx_chip[h, j, i] = (acc_chip[h, j, i] + rx_sib[h, j, i].astype(F32)).astype(BF16)
            p_chip(h, j).start()

    for h in range(heads):
        p_sib(h, 0).wait_recv()
        for link in links:
            there, _, here, _, col = link

            def add_edge(link=link, here=here, col=col, h=h):
                p_edge(h, link, True).wait_recv()
                for i in range(2):
                    for r in range(trows):
                        at = own_tile(r, col)
                        acc_own[h, i, at] += rx_edge[h, here, i, pl.ds(r * tile, tile)].astype(F32)
            guarded(there, add_edge)
        totals = [acc_own[h, i] + rx_sib[h, 0, i].astype(F32) for i in range(2)]
        for j in range(1, chips):
            p_chip(h, j).wait_recv()
            for i in range(2):
                totals[i] = totals[i] + rx_chip[h, j, i].astype(F32)
        out_ref[1, h] = totals[0].astype(BF16)
        out_ref[2, h] = totals[1].astype(BF16)

    for h in range(heads):
        kv_sib(h).wait_send()
        p_sib(h, 0).wait_send()
        for j in range(1, chips):
            kv_chip(h, j).wait_send()
            relay(h, j).wait_send()
            p_sib(h, j).wait_send()
            p_chip(h, j).wait_send()
        for link in links:
            def drain(link=link, h=h):
                for r in range(trows):
                    kv_edge(h, link, r).wait_send()
                p_edge(h, link).wait_send()
            guarded(link[0], drain)


def unstack(stacked, dq_hbm, dk_hbm, dv_hbm, sem):
    copies = [pltpu.make_async_copy(stacked.at[i], out, sem.at[i])
              for i, out in enumerate((dq_hbm, dk_hbm, dv_hbm))]
    for c in copies:
        c.start()
    for c in copies:
        c.wait()


def on_device(n_hb, n_wb, query_rows, key_rows, value_rows, grad_out, sel_tiles, sel_count, tile_radius):
    heads, trows, tcols, tile, depth = query_rows.shape
    picks = sel_tiles.shape[-1]
    rows = trows * tcols * tile
    chips = n_hb // 2
    sides = max(1, min(2, n_wb - 1))
    used = min(2, n_wb - 1)
    flat = (heads, rows, depth)
    keys = n_hb * rows + used * trows * tile
    dma = pltpu.SemaphoreType.DMA
    dims = (heads, trows, tcols, tile, picks, n_hb, n_wb, depth ** -0.5)
    hbm = pl.BlockSpec(memory_space=pltpu.HBM)
    smem = pl.BlockSpec(memory_space=pltpu.SMEM)
    vmem = pl.BlockSpec(memory_space=pltpu.VMEM)
    out = jax.ShapeDtypeStruct(flat, BF16)
    stacked = pl.pallas_call(
        functools.partial(kernel, dims),
        out_shape=pltpu.VMEM((3,) + flat, BF16),
        in_specs=[hbm] * 4 + [smem] * 3,
        out_specs=vmem,
        scratch_shapes=[
            pltpu.VMEM((2,) + flat, BF16),
            pltpu.VMEM((2, heads, keys, depth), BF16),
            pltpu.VMEM((heads, 2, rows, depth), F32),
            pltpu.VMEM((heads, chips, 2, rows, depth), F32),
            pltpu.VMEM((heads, chips, 2, rows, depth), BF16),
            pltpu.VMEM((heads, chips, 2, rows, depth), BF16),
            pltpu.VMEM((heads, chips, 2, rows, depth), BF16),
            pltpu.VMEM((heads, chips, 2, rows, depth), BF16),
            pltpu.VMEM((heads, sides, 2, trows * tile, depth), BF16),
            pltpu.VMEM((heads, sides, 2, trows * tile, depth), BF16),
            dma((2,)), dma((heads, 2)),
            dma((heads,)), dma((heads,)),
            dma((heads, chips)), dma((heads, chips)),
            dma((heads, chips)), dma((heads, chips)),
            dma((heads, sides, trows)), dma((heads, sides, trows)),
            dma((heads, chips)), dma((heads, chips)),
            dma((heads, chips)), dma((heads, chips)),
            dma((heads, sides)), dma((heads, sides)),
        ],
        compiler_params=pltpu.CompilerParams(
            collective_id=0, has_side_effects=True, vmem_limit_bytes=62 * 1024 * 1024),
        cost_estimate=pl.CostEstimate(
            flops=10 * heads * rows * keys * depth,
            bytes_accessed=14 * heads * rows * depth,
            transcendentals=heads * rows * keys),
    )(
        query_rows.reshape(flat), key_rows.reshape(flat), value_rows.reshape(flat),
        grad_out.reshape(flat), sel_tiles, sel_count.T, tile_radius,
    )
    results = pl.pallas_call(
        unstack,
        out_shape=(out, out, out),
        in_specs=[vmem],
        out_specs=(hbm,) * 3,
        scratch_shapes=[dma((3,))],
    )(stacked)
    return tuple(r.reshape(query_rows.shape) for r in results)


def solution(mesh):
    block = P("hd", "hb", "wb", None, None)
    return jax.shard_map(
        functools.partial(on_device, mesh.shape["hb"], mesh.shape["wb"]),
        mesh=mesh,
        in_specs=(block, block, block, block, P(None, "wb", None), P(None, "wb"), P("hd")),
        out_specs=(block, block, block),
        check_vma=False,
    )
```

```python
import functools

import jax
import jax.numpy as jnp
from jax import lax
from jax.experimental import pallas as pl
from jax.experimental.pallas import tpu as pltpu
from jax.sharding import PartitionSpec as P

MESH = pl.DeviceIdType.MESH
F32 = jnp.float32
BF16 = jnp.bfloat16
NT = (((1,), (1,)), ((), ()))
NN = (((1,), (0,)), ((), ()))
TN = (((0,), (0,)), ((), ()))


def dot(a, b, dims):
    return lax.dot_general(a, b, dims, preferred_element_type=F32)


def kernel(
    dims,
    q_hbm, k_hbm, v_hbm, g_hbm, sel_hbm, count_hbm, radius_hbm,
    out_ref,
    sel_ref, count_ref, radius_ref, qg, kv, acc_own, acc_chip, tx_sib, rx_sib, tx_chip, rx_chip, tx_edge, rx_edge,
    i_sem, q_sem, kv_sem, s_kvsib, r_kvsib, s_kvchip, r_kvchip, s_relay, r_relay, s_kvedge, r_kvedge,
    s_psib, r_psib, s_pchip, r_pchip, s_pedge, r_pedge,
):
    heads, trows, tcols, tile, picks, n_hb, n_wb, factor = dims
    rows = trows * tcols * tile
    chips = n_hb // 2
    me = lax.axis_index("hb")
    w = lax.axis_index("wb")
    chip, core = me // 2, me % 2
    sib = chip * 2 + 1 - core
    near_rows = 2 * rows + min(2, n_wb - 1) * trows * tile
    to_chip = {j: ((chip + j) % chips) * 2 + core for j in range(1, chips)}
    from_chip = {j: ((chip + chips - j) % chips) * 2 + core for j in range(1, chips)}
    if n_wb == 1:
        links = []
    elif n_wb == 2:
        links = [(None, 1 - w, 0, 0, (1 - w) * (tcols - 1))]
    else:
        links = [(w > 0, w - 1, 0, 1, 0), (w < n_wb - 1, w + 1, 1, 0, tcols - 1)]

    def guarded(there, fn):
        if there is None:
            fn()
        else:
            pl.when(there)(fn)

    def remote(src, dst, send, recv, axis, to):
        return pltpu.make_async_remote_copy(
            src_ref=src, dst_ref=dst, send_sem=send, recv_sem=recv,
            device_id={axis: to}, device_id_type=MESH,
        )

    own_kv = []
    for h in range(heads):
        own_kv.append((
            pltpu.make_async_copy(k_hbm.at[h], kv.at[0, h, pl.ds(0, rows)], kv_sem.at[h, 0]),
            pltpu.make_async_copy(v_hbm.at[h], kv.at[1, h, pl.ds(0, rows)], kv_sem.at[h, 1]),
        ))
        for c in own_kv[-1]:
            c.start()
    own_q = [
        pltpu.make_async_copy(q_hbm, qg.at[0], q_sem.at[0]),
        pltpu.make_async_copy(g_hbm, qg.at[1], q_sem.at[1]),
    ]
    indices = [
        pltpu.make_async_copy(src, dst, i_sem.at[i])
        for i, (src, dst) in enumerate(
            ((sel_hbm, sel_ref), (count_hbm, count_ref), (radius_hbm, radius_ref)))
    ]
    for c in own_q + indices:
        c.start()

    barrier = pltpu.get_barrier_semaphore()
    pl.semaphore_signal(barrier, inc=1, device_id={"hb": sib}, device_id_type=MESH)
    for j in range(1, chips):
        pl.semaphore_signal(barrier, inc=1, device_id={"hb": to_chip[j]}, device_id_type=MESH)
    for there, peer, _, _, _ in links:
        def hello(peer=peer):
            pl.semaphore_signal(barrier, inc=1, device_id={"wb": peer}, device_id_type=MESH)
        guarded(there, hello)
    if n_wb > 2:
        for slot, (there, _, _, _, _) in enumerate(links):
            def blank(slot=slot):
                at = 2 * rows + slot * trows * tile
                kv[:, :, pl.ds(at, trows * tile), :] = jnp.zeros(
                    (2, heads, trows * tile, kv.shape[-1]), BF16)
            pl.when(jnp.logical_not(there))(blank)
    greeted = chips
    for there, _, _, _, _ in links:
        greeted = greeted + (1 if there is None else jnp.where(there, 1, 0))
    pl.semaphore_wait(barrier, greeted)

    def slot_at(s):
        return pl.ds(s * rows if s < 2 else near_rows + (s - 2) * rows, rows)

    def edge_at(slot, r):
        return pl.ds(2 * rows + (slot * trows + r) * tile, tile)

    def kv_chip(h, j, i):
        return remote((k_hbm, v_hbm)[i].at[h], kv.at[i, h, slot_at(2 * j)],
                      s_kvchip.at[h, j, i], r_kvchip.at[h, j, i], "hb", to_chip[j])

    def kv_sib(h):
        return remote(kv.at[:, h, slot_at(0)], kv.at[:, h, slot_at(1)],
                      s_kvsib.at[h], r_kvsib.at[h], "hb", sib)

    def relay(h, j):
        return remote(kv.at[:, h, slot_at(2 * j)], kv.at[:, h, slot_at(2 * j + 1)],
                      s_relay.at[h, j], r_relay.at[h, j], "hb", sib)

    def own_tile(r, col):
        return pl.ds(pl.multiple_of((r * tcols + col) * tile, tile), tile)

    def kv_edge(h, link, r, arriving=False):
        _, peer, here, away, col = link
        slot = here if arriving else away
        return remote(kv.at[:, h, own_tile(r, col)], kv.at[:, h, edge_at(slot, r)],
                      s_kvedge.at[h, away, r], r_kvedge.at[h, slot, r], "wb", peer)

    def p_sib(h, j):
        return remote(tx_sib.at[h, j], rx_sib.at[h, j], s_psib.at[h, j], r_psib.at[h, j], "hb", sib)

    def p_chip(h, j):
        return remote(tx_chip.at[h, j], rx_chip.at[h, j],
                      s_pchip.at[h, j], r_pchip.at[h, j], "hb", from_chip[j])

    def p_edge(h, link, arriving=False):
        _, peer, here, away, _ = link
        slot = here if arriving else away
        return remote(tx_edge.at[h, here], rx_edge.at[h, slot],
                      s_pedge.at[h, here], r_pedge.at[h, slot], "wb", peer)

    for h in range(heads):
        for j in range(1, chips):
            for i in range(2):
                kv_chip(h, j, i).start()
    for h in range(heads):
        for c in own_kv[h]:
            c.wait()
        kv_sib(h).start()
        for link in links:
            def send(link=link, h=h):
                for r in range(trows):
                    kv_edge(h, link, r).start()
            guarded(link[0], send)

    for c in indices:
        c.wait()
    lane_tile = lax.broadcasted_iota(jnp.int32, (1, rows), 1) // tile
    lane_row = me * trows + lane_tile // tcols
    lane_col = lane_tile % tcols
    chosen = []
    for s in range(picks):
        entry = jnp.full((1, rows), -1, jnp.int32)
        for r in range(trows):
            for c in range(tcols):
                row = me * trows + r
                value = jnp.where(s < count_ref[c, row], sel_ref[row, c, s], -1)
                entry = jnp.where(lane_tile == r * tcols + c, value, entry)
        chosen.append(entry)
    spread, picked = [], []
    for s in range(n_hb):
        j = s // 2
        group = ((chip + chips - j) % chips) * 2 + (core if s % 2 == 0 else 1 - core)
        for r in range(trows):
            for c in range(tcols):
                key_row = group * trows + r
                spread.append(jnp.abs(lane_row - key_row) + jnp.abs(lane_col - c))
                at = key_row * tcols + c
                hit = functools.reduce(jnp.logical_or, [e == at for e in chosen])
                picked.append(hit)
    beside = []
    for there, _, slot, _, col in links:
        for r in range(trows):
            near = lane_tile == r * tcols + col
            if there is not None:
                near = jnp.logical_and(near, there)
            beside.append(near)

    for c in own_q:
        c.wait()

    near_tiles = 2 * trows * tcols

    def products(h, at):
        return dot(kv[0, h, at], qg[0, h], NT), dot(kv[1, h, at], qg[1, h], NT)

    def near_products(h):
        kv_sib(h).wait_recv()
        for link in links:
            def arrive(link=link):
                for r in range(trows):
                    kv_edge(h, link, r, True).wait_recv()
            guarded(link[0], arrive)
        return products(h, slice(0, near_rows))

    def softmax(h, blocks):
        radius = radius_ref[h]
        bias = [jnp.where(jnp.logical_or(sp <= radius, pk), 0.0, -jnp.inf)
                for sp, pk in zip(spread, picked)]
        edge = [jnp.where(jnp.logical_and(near, radius >= 1), 0.0, -jnp.inf) for near in beside]
        bias = bias[:near_tiles] + edge + bias[near_tiles:]
        s_t, d_t = [], []
        for scores, slopes in blocks:
            for i in range(scores.shape[0] // tile):
                cut = slice(i * tile, (i + 1) * tile)
                s_t.append(scores[cut] * factor + bias[len(s_t)])
                d_t.append(slopes[cut])
        top = jnp.max(functools.reduce(jnp.maximum, s_t), axis=0, keepdims=True)
        e_t = [jnp.exp(s - top) for s in s_t]
        total = jnp.sum(functools.reduce(jnp.add, e_t), axis=0, keepdims=True)
        mixed = jnp.sum(functools.reduce(jnp.add, [e * d for e, d in zip(e_t, d_t)]),
                        axis=0, keepdims=True)
        inverse = 1.0 / total
        delta = mixed * inverse
        probs = [e * inverse for e in e_t]
        half = jnp.concatenate([p.astype(BF16) for p in probs], axis=0)
        grad = jnp.concatenate(
            [(p * ((d - delta) * factor)).astype(BF16) for p, d in zip(probs, d_t)], axis=0)
        return half, grad

    def pass_on(h):
        for j in range(1, chips):
            for i in range(2):
                kv_chip(h, j, i).wait_recv()
            relay(h, j).start()

    blocks = [near_products(0)]
    pass_on(0)
    for h in range(heads):
        if chips > 1:
            for j in range(1, chips):
                relay(h, j).wait_recv()
            blocks.append(products(h, slice(near_rows, near_rows + (n_hb - 2) * rows)))
        half, grad = softmax(h, blocks)
        q, g = qg[0, h], qg[1, h]
        if chips > 1:
            far_parts = (dot(grad[near_rows:], q, NN), dot(half[near_rows:], g, NN))
            for j in range(1, chips):
                at = (2 * j - 2) * rows
                for i, part in enumerate(far_parts):
                    tx_sib[h, j, i] = part[at + rows:at + 2 * rows].astype(BF16)
                    acc_chip[h, j, i] = part[at:at + rows]
                p_sib(h, j).start()
        if h + 1 < heads:
            pass_on(h + 1)
        near_parts = (dot(grad[:near_rows], q, NN), dot(half[:near_rows], g, NN))
        for i, part in enumerate(near_parts):
            tx_sib[h, 0, i] = part[rows:2 * rows].astype(BF16)
            acc_own[h, i] = part[:rows]
        p_sib(h, 0).start()
        for link in links:
            at = 2 * rows + link[2] * trows * tile
            for i, part in enumerate(near_parts):
                tx_edge[h, link[2], i] = part[at:at + trows * tile].astype(BF16)
            guarded(link[0], lambda link=link, h=h: p_edge(h, link).start())
        out_ref[0, h] = dot(grad, kv[0, h], TN).astype(BF16)
        if h + 1 < heads:
            blocks = [near_products(h + 1)]
        for j in range(1, chips):
            p_sib(h, j).wait_recv()
            for i in range(2):
                tx_chip[h, j, i] = (acc_chip[h, j, i] + rx_sib[h, j, i].astype(F32)).astype(BF16)
            p_chip(h, j).start()

    for h in range(heads):
        p_sib(h, 0).wait_recv()
        for link in links:
            there, _, here, _, col = link

            def add_edge(link=link, here=here, col=col, h=h):
                p_edge(h, link, True).wait_recv()
                for i in range(2):
                    for r in range(trows):
                        at = own_tile(r, col)
                        acc_own[h, i, at] += rx_edge[h, here, i, pl.ds(r * tile, tile)].astype(F32)
            guarded(there, add_edge)
        totals = [acc_own[h, i] + rx_sib[h, 0, i].astype(F32) for i in range(2)]
        for j in range(1, chips):
            p_chip(h, j).wait_recv()
            for i in range(2):
                totals[i] = totals[i] + rx_chip[h, j, i].astype(F32)
        out_ref[1, h] = totals[0].astype(BF16)
        out_ref[2, h] = totals[1].astype(BF16)

    for h in range(heads):
        kv_sib(h).wait_send()
        p_sib(h, 0).wait_send()
        for j in range(1, chips):
            for i in range(2):
                kv_chip(h, j, i).wait_send()
            relay(h, j).wait_send()
            p_sib(h, j).wait_send()
            p_chip(h, j).wait_send()
        for link in links:
            def drain(link=link, h=h):
                for r in range(trows):
                    kv_edge(h, link, r).wait_send()
                p_edge(h, link).wait_send()
            guarded(link[0], drain)


def unstack(stacked, dq_hbm, dk_hbm, dv_hbm, sem):
    copies = [pltpu.make_async_copy(stacked.at[i], out, sem.at[i])
              for i, out in enumerate((dq_hbm, dk_hbm, dv_hbm))]
    for c in copies:
        c.start()
    for c in copies:
        c.wait()


def on_device(n_hb, n_wb, query_rows, key_rows, value_rows, grad_out, sel_tiles, sel_count, tile_radius):
    heads, trows, tcols, tile, depth = query_rows.shape
    picks = sel_tiles.shape[-1]
    rows = trows * tcols * tile
    chips = n_hb // 2
    sides = max(1, min(2, n_wb - 1))
    used = min(2, n_wb - 1)
    flat = (heads, rows, depth)
    keys = n_hb * rows + used * trows * tile
    dma = pltpu.SemaphoreType.DMA
    dims = (heads, trows, tcols, tile, picks, n_hb, n_wb, depth ** -0.5)
    hbm = pl.BlockSpec(memory_space=pltpu.HBM)
    vmem = pl.BlockSpec(memory_space=pltpu.VMEM)
    out = jax.ShapeDtypeStruct(flat, BF16)
    stacked = pl.pallas_call(
        functools.partial(kernel, dims),
        out_shape=pltpu.VMEM((3,) + flat, BF16),
        in_specs=[hbm] * 7,
        out_specs=vmem,
        scratch_shapes=[
            pltpu.SMEM(sel_tiles.shape, jnp.int32),
            pltpu.SMEM(sel_count.shape[::-1], jnp.int32),
            pltpu.SMEM(tile_radius.shape, jnp.int32),
            pltpu.VMEM((2,) + flat, BF16),
            pltpu.VMEM((2, heads, keys, depth), BF16),
            pltpu.VMEM((heads, 2, rows, depth), F32),
            pltpu.VMEM((heads, chips, 2, rows, depth), F32),
            pltpu.VMEM((heads, chips, 2, rows, depth), BF16),
            pltpu.VMEM((heads, chips, 2, rows, depth), BF16),
            pltpu.VMEM((heads, chips, 2, rows, depth), BF16),
            pltpu.VMEM((heads, chips, 2, rows, depth), BF16),
            pltpu.VMEM((heads, sides, 2, trows * tile, depth), BF16),
            pltpu.VMEM((heads, sides, 2, trows * tile, depth), BF16),
            dma((3,)), dma((2,)), dma((heads, 2)),
            dma((heads,)), dma((heads,)),
            dma((heads, chips, 2)), dma((heads, chips, 2)),
            dma((heads, chips)), dma((heads, chips)),
            dma((heads, sides, trows)), dma((heads, sides, trows)),
            dma((heads, chips)), dma((heads, chips)),
            dma((heads, chips)), dma((heads, chips)),
            dma((heads, sides)), dma((heads, sides)),
        ],
        compiler_params=pltpu.CompilerParams(
            collective_id=0, has_side_effects=True, vmem_limit_bytes=62 * 1024 * 1024),
        cost_estimate=pl.CostEstimate(
            flops=10 * heads * rows * keys * depth,
            bytes_accessed=14 * heads * rows * depth,
            transcendentals=heads * rows * keys),
    )(
        query_rows.reshape(flat), key_rows.reshape(flat), value_rows.reshape(flat),
        grad_out.reshape(flat), sel_tiles, sel_count.T, tile_radius,
    )
    results = pl.pallas_call(
        unstack,
        out_shape=(out, out, out),
        in_specs=[vmem],
        out_specs=(hbm,) * 3,
        scratch_shapes=[dma((3,))],
        compiler_params=pltpu.CompilerParams(vmem_limit_bytes=1024 * 1024),
    )(stacked)
    return tuple(r.reshape(query_rows.shape) for r in results)


def solution(mesh):
    block = P("hd", "hb", "wb", None, None)
    return jax.shard_map(
        functools.partial(on_device, mesh.shape["hb"], mesh.shape["wb"]),
        mesh=mesh,
        in_specs=(block, block, block, block, P(None, "wb", None), P(None, "wb"), P("hd")),
        out_specs=(block, block, block),
        check_vma=False,
    )
```

```python
import functools

import jax
import jax.numpy as jnp
from jax import lax
from jax.experimental import pallas as pl
from jax.experimental.pallas import tpu as pltpu
from jax.sharding import PartitionSpec as P

MESH = pl.DeviceIdType.MESH
F32 = jnp.float32
BF16 = jnp.bfloat16
NT = (((1,), (1,)), ((), ()))
NN = (((1,), (0,)), ((), ()))
TN = (((0,), (0,)), ((), ()))


def dot(a, b, dims):
    return lax.dot_general(a, b, dims, preferred_element_type=F32)


def kernel(
    dims,
    q_hbm, k_hbm, v_hbm, g_hbm, sel_hbm, count_hbm, radius_hbm,
    out_ref,
    sel_ref, count_ref, radius_ref, qg, kv, acc_own, acc_chip, tx_sib, rx_sib, tx_chip, rx_chip, tx_edge, rx_edge,
    i_sem, q_sem, kv_sem, s_kvsib, r_kvsib, s_kvchip, r_kvchip, s_relay, r_relay, s_kvedge, r_kvedge,
    s_psib, r_psib, s_pchip, r_pchip, s_pedge, r_pedge,
):
    heads, trows, tcols, tile, picks, n_hb, n_wb, factor = dims
    rows = trows * tcols * tile
    chips = n_hb // 2
    me = lax.axis_index("hb")
    w = lax.axis_index("wb")
    chip, core = me // 2, me % 2
    sib = chip * 2 + 1 - core
    near_rows = 2 * rows + min(2, n_wb - 1) * trows * tile
    to_chip = {j: ((chip + j) % chips) * 2 + core for j in range(1, chips)}
    from_chip = {j: ((chip + chips - j) % chips) * 2 + core for j in range(1, chips)}
    if n_wb == 1:
        links = []
    elif n_wb == 2:
        links = [(None, 1 - w, 0, 0, (1 - w) * (tcols - 1))]
    else:
        links = [(w > 0, w - 1, 0, 1, 0), (w < n_wb - 1, w + 1, 1, 0, tcols - 1)]

    def guarded(there, fn):
        if there is None:
            fn()
        else:
            pl.when(there)(fn)

    def remote(src, dst, send, recv, axis, to):
        return pltpu.make_async_remote_copy(
            src_ref=src, dst_ref=dst, send_sem=send, recv_sem=recv,
            device_id={axis: to}, device_id_type=MESH,
        )

    own_kv = []
    for h in range(heads):
        own_kv.append((
            pltpu.make_async_copy(k_hbm.at[h], kv.at[0, h, pl.ds(0, rows)], kv_sem.at[h, 0]),
            pltpu.make_async_copy(v_hbm.at[h], kv.at[1, h, pl.ds(0, rows)], kv_sem.at[h, 1]),
        ))
        for c in own_kv[-1]:
            c.start()
    own_q = [
        pltpu.make_async_copy(q_hbm, qg.at[0], q_sem.at[0]),
        pltpu.make_async_copy(g_hbm, qg.at[1], q_sem.at[1]),
    ]
    indices = [
        pltpu.make_async_copy(src, dst, i_sem.at[i])
        for i, (src, dst) in enumerate(
            ((sel_hbm, sel_ref), (count_hbm, count_ref), (radius_hbm, radius_ref)))
    ]
    for c in own_q + indices:
        c.start()

    barrier = pltpu.get_barrier_semaphore()
    pl.semaphore_signal(barrier, inc=1, device_id={"hb": sib}, device_id_type=MESH)
    for j in range(1, chips):
        pl.semaphore_signal(barrier, inc=1, device_id={"hb": to_chip[j]}, device_id_type=MESH)
    for there, peer, _, _, _ in links:
        def hello(peer=peer):
            pl.semaphore_signal(barrier, inc=1, device_id={"wb": peer}, device_id_type=MESH)
        guarded(there, hello)
    if n_wb > 2:
        for slot, (there, _, _, _, _) in enumerate(links):
            def blank(slot=slot):
                at = 2 * rows + slot * trows * tile
                kv[:, :, pl.ds(at, trows * tile), :] = jnp.zeros(
                    (2, heads, trows * tile, kv.shape[-1]), BF16)
            pl.when(jnp.logical_not(there))(blank)
    greeted = chips
    for there, _, _, _, _ in links:
        greeted = greeted + (1 if there is None else jnp.where(there, 1, 0))
    pl.semaphore_wait(barrier, greeted)

    def slot_at(s):
        return pl.ds(s * rows if s < 2 else near_rows + (s - 2) * rows, rows)

    def edge_at(slot, r):
        return pl.ds(2 * rows + (slot * trows + r) * tile, tile)

    def kv_chip(h, j, i):
        return remote((k_hbm, v_hbm)[i].at[h], kv.at[i, h, slot_at(2 * j)],
                      s_kvchip.at[h, j, i], r_kvchip.at[h, j, i], "hb", to_chip[j])

    def kv_sib(h):
        return remote(kv.at[:, h, slot_at(0)], kv.at[:, h, slot_at(1)],
                      s_kvsib.at[h], r_kvsib.at[h], "hb", sib)

    def relay(h, j):
        return remote(kv.at[:, h, slot_at(2 * j)], kv.at[:, h, slot_at(2 * j + 1)],
                      s_relay.at[h, j], r_relay.at[h, j], "hb", sib)

    def own_tile(r, col):
        return pl.ds(pl.multiple_of((r * tcols + col) * tile, tile), tile)

    def kv_edge(h, link, r, arriving=False):
        _, peer, here, away, col = link
        slot = here if arriving else away
        return remote(kv.at[:, h, own_tile(r, col)], kv.at[:, h, edge_at(slot, r)],
                      s_kvedge.at[h, away, r], r_kvedge.at[h, slot, r], "wb", peer)

    def p_sib(h, j):
        return remote(tx_sib.at[h, j], rx_sib.at[h, j], s_psib.at[h, j], r_psib.at[h, j], "hb", sib)

    def p_chip(h, j):
        return remote(tx_chip.at[h, j], rx_chip.at[h, j],
                      s_pchip.at[h, j], r_pchip.at[h, j], "hb", from_chip[j])

    def p_edge(h, link, arriving=False):
        _, peer, here, away, _ = link
        slot = here if arriving else away
        return remote(tx_edge.at[h, here], rx_edge.at[h, slot],
                      s_pedge.at[h, here], r_pedge.at[h, slot], "wb", peer)

    def send_chip(h):
        for j in range(1, chips):
            for i in range(2):
                if h:
                    kv_chip(h - 1, j, i).wait_send()
                kv_chip(h, j, i).start()

    send_chip(0)
    for h in range(heads):
        for c in own_kv[h]:
            c.wait()
        kv_sib(h).start()
        for link in links:
            def send(link=link, h=h):
                for r in range(trows):
                    kv_edge(h, link, r).start()
            guarded(link[0], send)

    for c in indices:
        c.wait()
    lane_tile = lax.broadcasted_iota(jnp.int32, (1, rows), 1) // tile
    lane_row = me * trows + lane_tile // tcols
    lane_col = lane_tile % tcols
    chosen = []
    for s in range(picks):
        entry = jnp.full((1, rows), -1, jnp.int32)
        for r in range(trows):
            for c in range(tcols):
                row = me * trows + r
                value = jnp.where(s < count_ref[c, row], sel_ref[row, c, s], -1)
                entry = jnp.where(lane_tile == r * tcols + c, value, entry)
        chosen.append(entry)
    spread, picked = [], []
    for s in range(n_hb):
        j = s // 2
        group = ((chip + chips - j) % chips) * 2 + (core if s % 2 == 0 else 1 - core)
        for r in range(trows):
            for c in range(tcols):
                key_row = group * trows + r
                spread.append(jnp.abs(lane_row - key_row) + jnp.abs(lane_col - c))
                at = key_row * tcols + c
                hit = functools.reduce(jnp.logical_or, [e == at for e in chosen])
                picked.append(hit)
    beside = []
    for there, _, slot, _, col in links:
        for r in range(trows):
            near = lane_tile == r * tcols + col
            if there is not None:
                near = jnp.logical_and(near, there)
            beside.append(near)

    for c in own_q:
        c.wait()

    near_tiles = 2 * trows * tcols

    def products(h, at):
        return dot(kv[0, h, at], qg[0, h], NT), dot(kv[1, h, at], qg[1, h], NT)

    def near_products(h):
        kv_sib(h).wait_recv()
        for link in links:
            def arrive(link=link):
                for r in range(trows):
                    kv_edge(h, link, r, True).wait_recv()
            guarded(link[0], arrive)
        return products(h, slice(0, near_rows))

    def softmax(h, blocks):
        radius = radius_ref[h]
        bias = [jnp.where(jnp.logical_or(sp <= radius, pk), 0.0, -jnp.inf)
                for sp, pk in zip(spread, picked)]
        edge = [jnp.where(jnp.logical_and(near, radius >= 1), 0.0, -jnp.inf) for near in beside]
        bias = bias[:near_tiles] + edge + bias[near_tiles:]
        s_t, d_t = [], []
        for scores, slopes in blocks:
            for i in range(scores.shape[0] // tile):
                cut = slice(i * tile, (i + 1) * tile)
                s_t.append(scores[cut] * factor + bias[len(s_t)])
                d_t.append(slopes[cut])
        top = jnp.max(functools.reduce(jnp.maximum, s_t), axis=0, keepdims=True)
        e_t = [jnp.exp(s - top) for s in s_t]
        total = jnp.sum(functools.reduce(jnp.add, e_t), axis=0, keepdims=True)
        mixed = jnp.sum(functools.reduce(jnp.add, [e * d for e, d in zip(e_t, d_t)]),
                        axis=0, keepdims=True)
        inverse = 1.0 / total
        delta = mixed * inverse
        probs = [e * inverse for e in e_t]
        half = jnp.concatenate([p.astype(BF16) for p in probs], axis=0)
        grad = jnp.concatenate(
            [(p * ((d - delta) * factor)).astype(BF16) for p, d in zip(probs, d_t)], axis=0)
        return half, grad

    def pass_on(h):
        for j in range(1, chips):
            for i in range(2):
                kv_chip(h, j, i).wait_recv()
            relay(h, j).start()

    blocks = [near_products(0)]
    if heads > 1:
        send_chip(1)
    pass_on(0)
    for h in range(heads):
        if h + 2 < heads:
            send_chip(h + 2)
        if chips > 1:
            for j in range(1, chips):
                relay(h, j).wait_recv()
            blocks.append(products(h, slice(near_rows, near_rows + (n_hb - 2) * rows)))
        half, grad = softmax(h, blocks)
        q, g = qg[0, h], qg[1, h]
        if chips > 1:
            far_parts = (dot(grad[near_rows:], q, NN), dot(half[near_rows:], g, NN))
            for j in range(1, chips):
                at = (2 * j - 2) * rows
                for i, part in enumerate(far_parts):
                    tx_sib[h, j, i] = part[at + rows:at + 2 * rows].astype(BF16)
                    acc_chip[h, j, i] = part[at:at + rows]
                p_sib(h, j).start()
        if h + 1 < heads:
            pass_on(h + 1)
        near_parts = (dot(grad[:near_rows], q, NN), dot(half[:near_rows], g, NN))
        for i, part in enumerate(near_parts):
            tx_sib[h, 0, i] = part[rows:2 * rows].astype(BF16)
            acc_own[h, i] = part[:rows]
        p_sib(h, 0).start()
        for link in links:
            at = 2 * rows + link[2] * trows * tile
            for i, part in enumerate(near_parts):
                tx_edge[h, link[2], i] = part[at:at + trows * tile].astype(BF16)
            guarded(link[0], lambda link=link, h=h: p_edge(h, link).start())
        out_ref[0, h] = dot(grad, kv[0, h], TN).astype(BF16)
        if h + 1 < heads:
            blocks = [near_products(h + 1)]
        for j in range(1, chips):
            p_sib(h, j).wait_recv()
            for i in range(2):
                tx_chip[h, j, i] = (acc_chip[h, j, i] + rx_sib[h, j, i].astype(F32)).astype(BF16)
            p_chip(h, j).start()

    for h in range(heads):
        p_sib(h, 0).wait_recv()
        for link in links:
            there, _, here, _, col = link

            def add_edge(link=link, here=here, col=col, h=h):
                p_edge(h, link, True).wait_recv()
                for i in range(2):
                    for r in range(trows):
                        at = own_tile(r, col)
                        acc_own[h, i, at] += rx_edge[h, here, i, pl.ds(r * tile, tile)].astype(F32)
            guarded(there, add_edge)
        totals = [acc_own[h, i] + rx_sib[h, 0, i].astype(F32) for i in range(2)]
        for j in range(1, chips):
            p_chip(h, j).wait_recv()
            for i in range(2):
                totals[i] = totals[i] + rx_chip[h, j, i].astype(F32)
        out_ref[1, h] = totals[0].astype(BF16)
        out_ref[2, h] = totals[1].astype(BF16)

    for h in range(heads):
        kv_sib(h).wait_send()
        p_sib(h, 0).wait_send()
        for j in range(1, chips):
            if h == heads - 1:
                for i in range(2):
                    kv_chip(h, j, i).wait_send()
            relay(h, j).wait_send()
            p_sib(h, j).wait_send()
            p_chip(h, j).wait_send()
        for link in links:
            def drain(link=link, h=h):
                for r in range(trows):
                    kv_edge(h, link, r).wait_send()
                p_edge(h, link).wait_send()
            guarded(link[0], drain)


def unstack(stacked, dq_hbm, dk_hbm, dv_hbm, sem):
    copies = [pltpu.make_async_copy(stacked.at[i], out, sem.at[i])
              for i, out in enumerate((dq_hbm, dk_hbm, dv_hbm))]
    for c in copies:
        c.start()
    for c in copies:
        c.wait()


def on_device(n_hb, n_wb, query_rows, key_rows, value_rows, grad_out, sel_tiles, sel_count, tile_radius):
    heads, trows, tcols, tile, depth = query_rows.shape
    picks = sel_tiles.shape[-1]
    rows = trows * tcols * tile
    chips = n_hb // 2
    sides = max(1, min(2, n_wb - 1))
    used = min(2, n_wb - 1)
    flat = (heads, rows, depth)
    keys = n_hb * rows + used * trows * tile
    dma = pltpu.SemaphoreType.DMA
    dims = (heads, trows, tcols, tile, picks, n_hb, n_wb, depth ** -0.5)
    hbm = pl.BlockSpec(memory_space=pltpu.HBM)
    vmem = pl.BlockSpec(memory_space=pltpu.VMEM)
    out = jax.ShapeDtypeStruct(flat, BF16)
    stacked = pl.pallas_call(
        functools.partial(kernel, dims),
        out_shape=pltpu.VMEM((3,) + flat, BF16),
        in_specs=[hbm] * 7,
        out_specs=vmem,
        scratch_shapes=[
            pltpu.SMEM(sel_tiles.shape, jnp.int32),
            pltpu.SMEM(sel_count.shape[::-1], jnp.int32),
            pltpu.SMEM(tile_radius.shape, jnp.int32),
            pltpu.VMEM((2,) + flat, BF16),
            pltpu.VMEM((2, heads, keys, depth), BF16),
            pltpu.VMEM((heads, 2, rows, depth), F32),
            pltpu.VMEM((heads, chips, 2, rows, depth), F32),
            pltpu.VMEM((heads, chips, 2, rows, depth), BF16),
            pltpu.VMEM((heads, chips, 2, rows, depth), BF16),
            pltpu.VMEM((heads, chips, 2, rows, depth), BF16),
            pltpu.VMEM((heads, chips, 2, rows, depth), BF16),
            pltpu.VMEM((heads, sides, 2, trows * tile, depth), BF16),
            pltpu.VMEM((heads, sides, 2, trows * tile, depth), BF16),
            dma((3,)), dma((2,)), dma((heads, 2)),
            dma((heads,)), dma((heads,)),
            dma((heads, chips, 2)), dma((heads, chips, 2)),
            dma((heads, chips)), dma((heads, chips)),
            dma((heads, sides, trows)), dma((heads, sides, trows)),
            dma((heads, chips)), dma((heads, chips)),
            dma((heads, chips)), dma((heads, chips)),
            dma((heads, sides)), dma((heads, sides)),
        ],
        compiler_params=pltpu.CompilerParams(
            collective_id=0, has_side_effects=True, vmem_limit_bytes=62 * 1024 * 1024),
        cost_estimate=pl.CostEstimate(
            flops=10 * heads * rows * keys * depth,
            bytes_accessed=14 * heads * rows * depth,
            transcendentals=heads * rows * keys),
    )(
        query_rows.reshape(flat), key_rows.reshape(flat), value_rows.reshape(flat),
        grad_out.reshape(flat), sel_tiles, sel_count.T, tile_radius,
    )
    results = pl.pallas_call(
        unstack,
        out_shape=(out, out, out),
        in_specs=[vmem],
        out_specs=(hbm,) * 3,
        scratch_shapes=[dma((3,))],
        compiler_params=pltpu.CompilerParams(vmem_limit_bytes=1024 * 1024),
    )(stacked)
    return tuple(r.reshape(query_rows.shape) for r in results)


def solution(mesh):
    block = P("hd", "hb", "wb", None, None)
    return jax.shard_map(
        functools.partial(on_device, mesh.shape["hb"], mesh.shape["wb"]),
        mesh=mesh,
        in_specs=(block, block, block, block, P(None, "wb", None), P(None, "wb"), P("hd")),
        out_specs=(block, block, block),
        check_vma=False,
    )
```

```python
import functools

import jax
import jax.numpy as jnp
from jax import lax
from jax.experimental import pallas as pl
from jax.experimental.pallas import tpu as pltpu
from jax.sharding import PartitionSpec as P

MESH = pl.DeviceIdType.MESH
F32 = jnp.float32
BF16 = jnp.bfloat16
NT = (((1,), (1,)), ((), ()))
NN = (((1,), (0,)), ((), ()))
TN = (((0,), (0,)), ((), ()))


def dot(a, b, dims):
    return lax.dot_general(a, b, dims, preferred_element_type=F32)


def kernel(
    dims,
    q_hbm, k_hbm, v_hbm, g_hbm, sel_hbm, count_hbm, radius_hbm,
    out_ref,
    sel_ref, count_ref, radius_ref, qg, kv, acc_own, acc_chip, tx_sib, rx_sib, tx_chip, rx_chip, tx_edge, rx_edge,
    i_sem, q_sem, kv_sem, s_kvsib, r_kvsib, s_kvchip, r_kvchip, s_relay, r_relay, s_kvedge, r_kvedge,
    s_psib, r_psib, s_pchip, r_pchip, s_pedge, r_pedge,
):
    heads, trows, tcols, tile, picks, n_hb, n_wb, factor = dims
    rows = trows * tcols * tile
    chips = n_hb // 2
    me = lax.axis_index("hb")
    w = lax.axis_index("wb")
    chip, core = me // 2, me % 2
    sib = chip * 2 + 1 - core
    near_rows = 2 * rows + min(2, n_wb - 1) * trows * tile
    to_chip = {j: ((chip + j) % chips) * 2 + core for j in range(1, chips)}
    from_chip = {j: ((chip + chips - j) % chips) * 2 + core for j in range(1, chips)}
    if n_wb == 1:
        links = []
    elif n_wb == 2:
        links = [(None, 1 - w, 0, 0, (1 - w) * (tcols - 1))]
    else:
        links = [(w > 0, w - 1, 0, 1, 0), (w < n_wb - 1, w + 1, 1, 0, tcols - 1)]

    def guarded(there, fn):
        if there is None:
            fn()
        else:
            pl.when(there)(fn)

    def remote(src, dst, send, recv, axis, to):
        return pltpu.make_async_remote_copy(
            src_ref=src, dst_ref=dst, send_sem=send, recv_sem=recv,
            device_id={axis: to}, device_id_type=MESH,
        )

    own_kv = []
    for h in range(heads):
        own_kv.append((
            pltpu.make_async_copy(k_hbm.at[h], kv.at[0, h, pl.ds(0, rows)], kv_sem.at[h, 0]),
            pltpu.make_async_copy(v_hbm.at[h], kv.at[1, h, pl.ds(0, rows)], kv_sem.at[h, 1]),
        ))
        for c in own_kv[-1]:
            c.start()
    own_q = [
        pltpu.make_async_copy(q_hbm, qg.at[0], q_sem.at[0]),
        pltpu.make_async_copy(g_hbm, qg.at[1], q_sem.at[1]),
    ]
    indices = [
        pltpu.make_async_copy(src, dst, i_sem.at[i])
        for i, (src, dst) in enumerate(
            ((sel_hbm, sel_ref), (count_hbm, count_ref), (radius_hbm, radius_ref)))
    ]
    for c in own_q + indices:
        c.start()

    barrier = pltpu.get_barrier_semaphore()
    pl.semaphore_signal(barrier, inc=1, device_id={"hb": sib}, device_id_type=MESH)
    for j in range(1, chips):
        pl.semaphore_signal(barrier, inc=1, device_id={"hb": to_chip[j]}, device_id_type=MESH)
    for there, peer, _, _, _ in links:
        def hello(peer=peer):
            pl.semaphore_signal(barrier, inc=1, device_id={"wb": peer}, device_id_type=MESH)
        guarded(there, hello)
    if n_wb > 2:
        for slot, (there, _, _, _, _) in enumerate(links):
            def blank(slot=slot):
                at = 2 * rows + slot * trows * tile
                kv[:, :, pl.ds(at, trows * tile), :] = jnp.zeros(
                    (2, heads, trows * tile, kv.shape[-1]), BF16)
            pl.when(jnp.logical_not(there))(blank)
    greeted = chips
    for there, _, _, _, _ in links:
        greeted = greeted + (1 if there is None else jnp.where(there, 1, 0))
    pl.semaphore_wait(barrier, greeted)

    def slot_at(s):
        return pl.ds(s * rows if s < 2 else near_rows + (s - 2) * rows, rows)

    def edge_at(slot, r):
        return pl.ds(2 * rows + (slot * trows + r) * tile, tile)

    def kv_chip(h, j, i):
        return remote((k_hbm, v_hbm)[i].at[h], kv.at[i, h, slot_at(2 * j)],
                      s_kvchip.at[h, j, i], r_kvchip.at[h, j, i], "hb", to_chip[j])

    def kv_sib(h):
        return remote(kv.at[:, h, slot_at(0)], kv.at[:, h, slot_at(1)],
                      s_kvsib.at[h], r_kvsib.at[h], "hb", sib)

    def relay(h, j, i):
        return remote(kv.at[i, h, slot_at(2 * j)], kv.at[i, h, slot_at(2 * j + 1)],
                      s_relay.at[h, j, i], r_relay.at[h, j, i], "hb", sib)

    def own_tile(r, col):
        return pl.ds(pl.multiple_of((r * tcols + col) * tile, tile), tile)

    def kv_edge(h, link, r, arriving=False):
        _, peer, here, away, col = link
        slot = here if arriving else away
        return remote(kv.at[:, h, own_tile(r, col)], kv.at[:, h, edge_at(slot, r)],
                      s_kvedge.at[h, away, r], r_kvedge.at[h, slot, r], "wb", peer)

    def p_sib(h, j, i):
        return remote(tx_sib.at[h, j, i], rx_sib.at[h, j, i],
                      s_psib.at[h, j, i], r_psib.at[h, j, i], "hb", sib)

    def p_chip(h, j, i):
        return remote(tx_chip.at[h, j, i], rx_chip.at[h, j, i],
                      s_pchip.at[h, j, i], r_pchip.at[h, j, i], "hb", from_chip[j])

    def p_edge(h, link, arriving=False):
        _, peer, here, away, _ = link
        slot = here if arriving else away
        return remote(tx_edge.at[h, here], rx_edge.at[h, slot],
                      s_pedge.at[h, here], r_pedge.at[h, slot], "wb", peer)

    for h in range(heads):
        for j in range(1, chips):
            for i in range(2):
                kv_chip(h, j, i).start()
    for h in range(heads):
        for c in own_kv[h]:
            c.wait()
        kv_sib(h).start()
        for link in links:
            def send(link=link, h=h):
                for r in range(trows):
                    kv_edge(h, link, r).start()
            guarded(link[0], send)

    for c in indices:
        c.wait()
    lane_tile = lax.broadcasted_iota(jnp.int32, (1, rows), 1) // tile
    lane_row = me * trows + lane_tile // tcols
    lane_col = lane_tile % tcols
    chosen = []
    for s in range(picks):
        entry = jnp.full((1, rows), -1, jnp.int32)
        for r in range(trows):
            for c in range(tcols):
                row = me * trows + r
                value = jnp.where(s < count_ref[c, row], sel_ref[row, c, s], -1)
                entry = jnp.where(lane_tile == r * tcols + c, value, entry)
        chosen.append(entry)
    spread, picked = [], []
    for s in range(n_hb):
        j = s // 2
        group = ((chip + chips - j) % chips) * 2 + (core if s % 2 == 0 else 1 - core)
        for r in range(trows):
            for c in range(tcols):
                key_row = group * trows + r
                spread.append(jnp.abs(lane_row - key_row) + jnp.abs(lane_col - c))
                at = key_row * tcols + c
                hit = functools.reduce(jnp.logical_or, [e == at for e in chosen])
                picked.append(hit)
    beside = []
    for there, _, slot, _, col in links:
        for r in range(trows):
            near = lane_tile == r * tcols + col
            if there is not None:
                near = jnp.logical_and(near, there)
            beside.append(near)

    for c in own_q:
        c.wait()

    near_tiles = 2 * trows * tcols

    def product(i, h, at):
        return dot(kv[i, h, at], qg[i, h], NT)

    def near_products(h):
        kv_sib(h).wait_recv()
        for link in links:
            def arrive(link=link):
                for r in range(trows):
                    kv_edge(h, link, r, True).wait_recv()
            guarded(link[0], arrive)
        return [product(i, h, slice(0, near_rows)) for i in range(2)]

    def softmax(h, blocks):
        radius = radius_ref[h]
        bias = [jnp.where(jnp.logical_or(sp <= radius, pk), 0.0, -jnp.inf)
                for sp, pk in zip(spread, picked)]
        edge = [jnp.where(jnp.logical_and(near, radius >= 1), 0.0, -jnp.inf) for near in beside]
        bias = bias[:near_tiles] + edge + bias[near_tiles:]
        s_t, d_t = [], []
        for scores, slopes in blocks:
            for i in range(scores.shape[0] // tile):
                cut = slice(i * tile, (i + 1) * tile)
                s_t.append(scores[cut] * factor + bias[len(s_t)])
                d_t.append(slopes[cut])
        top = jnp.max(functools.reduce(jnp.maximum, s_t), axis=0, keepdims=True)
        e_t = [jnp.exp(s - top) for s in s_t]
        total = jnp.sum(functools.reduce(jnp.add, e_t), axis=0, keepdims=True)
        mixed = jnp.sum(functools.reduce(jnp.add, [e * d for e, d in zip(e_t, d_t)]),
                        axis=0, keepdims=True)
        inverse = 1.0 / total
        delta = mixed * inverse
        probs = [e * inverse for e in e_t]
        half = jnp.concatenate([p.astype(BF16) for p in probs], axis=0)
        grad = jnp.concatenate(
            [(p * ((d - delta) * factor)).astype(BF16) for p, d in zip(probs, d_t)], axis=0)
        return half, grad

    def pass_on(h):
        for i in range(2):
            for j in range(1, chips):
                kv_chip(h, j, i).wait_recv()
                relay(h, j, i).start()

    blocks = [near_products(0)]
    pass_on(0)
    for h in range(heads):
        if chips > 1:
            far = []
            for i in range(2):
                for j in range(1, chips):
                    relay(h, j, i).wait_recv()
                far.append(product(i, h, slice(near_rows, near_rows + (n_hb - 2) * rows)))
            blocks.append(far)
        half, grad = softmax(h, blocks)
        q, g = qg[0, h], qg[1, h]
        if chips > 1:
            for i in (1, 0):
                part = dot((grad, half)[i][near_rows:], (q, g)[i], NN)
                for j in range(1, chips):
                    at = (2 * j - 2) * rows
                    tx_sib[h, j, i] = part[at + rows:at + 2 * rows].astype(BF16)
                    acc_chip[h, j, i] = part[at:at + rows]
                    p_sib(h, j, i).start()
        if h + 1 < heads:
            pass_on(h + 1)
        near_parts = (dot(grad[:near_rows], q, NN), dot(half[:near_rows], g, NN))
        for i, part in enumerate(near_parts):
            tx_sib[h, 0, i] = part[rows:2 * rows].astype(BF16)
            acc_own[h, i] = part[:rows]
            p_sib(h, 0, i).start()
        for link in links:
            at = 2 * rows + link[2] * trows * tile
            for i, part in enumerate(near_parts):
                tx_edge[h, link[2], i] = part[at:at + trows * tile].astype(BF16)
            guarded(link[0], lambda link=link, h=h: p_edge(h, link).start())
        out_ref[0, h] = dot(grad, kv[0, h], TN).astype(BF16)
        if h + 1 < heads:
            blocks = [near_products(h + 1)]
        for i in (1, 0):
            for j in range(1, chips):
                p_sib(h, j, i).wait_recv()
                tx_chip[h, j, i] = (acc_chip[h, j, i] + rx_sib[h, j, i].astype(F32)).astype(BF16)
                p_chip(h, j, i).start()

    for h in range(heads):
        for i in range(2):
            p_sib(h, 0, i).wait_recv()
        for link in links:
            there, _, here, _, col = link

            def add_edge(link=link, here=here, col=col, h=h):
                p_edge(h, link, True).wait_recv()
                for i in range(2):
                    for r in range(trows):
                        at = own_tile(r, col)
                        acc_own[h, i, at] += rx_edge[h, here, i, pl.ds(r * tile, tile)].astype(F32)
            guarded(there, add_edge)
        totals = [acc_own[h, i] + rx_sib[h, 0, i].astype(F32) for i in range(2)]
        for i in (1, 0):
            for j in range(1, chips):
                p_chip(h, j, i).wait_recv()
                totals[i] = totals[i] + rx_chip[h, j, i].astype(F32)
            out_ref[1 + i, h] = totals[i].astype(BF16)

    for h in range(heads):
        kv_sib(h).wait_send()
        for i in range(2):
            p_sib(h, 0, i).wait_send()
            for j in range(1, chips):
                for copy in (kv_chip, relay, p_sib, p_chip):
                    copy(h, j, i).wait_send()
        for link in links:
            def drain(link=link, h=h):
                for r in range(trows):
                    kv_edge(h, link, r).wait_send()
                p_edge(h, link).wait_send()
            guarded(link[0], drain)


def unstack(stacked, dq_hbm, dk_hbm, dv_hbm, sem):
    copies = [pltpu.make_async_copy(stacked.at[i], out, sem.at[i])
              for i, out in enumerate((dq_hbm, dk_hbm, dv_hbm))]
    for c in copies:
        c.start()
    for c in copies:
        c.wait()


def on_device(n_hb, n_wb, query_rows, key_rows, value_rows, grad_out, sel_tiles, sel_count, tile_radius):
    heads, trows, tcols, tile, depth = query_rows.shape
    picks = sel_tiles.shape[-1]
    rows = trows * tcols * tile
    chips = n_hb // 2
    sides = max(1, min(2, n_wb - 1))
    used = min(2, n_wb - 1)
    flat = (heads, rows, depth)
    keys = n_hb * rows + used * trows * tile
    dma = pltpu.SemaphoreType.DMA
    dims = (heads, trows, tcols, tile, picks, n_hb, n_wb, depth ** -0.5)
    hbm = pl.BlockSpec(memory_space=pltpu.HBM)
    vmem = pl.BlockSpec(memory_space=pltpu.VMEM)
    out = jax.ShapeDtypeStruct(flat, BF16)
    stacked = pl.pallas_call(
        functools.partial(kernel, dims),
        out_shape=pltpu.VMEM((3,) + flat, BF16),
        in_specs=[hbm] * 7,
        out_specs=vmem,
        scratch_shapes=[
            pltpu.SMEM(sel_tiles.shape, jnp.int32),
            pltpu.SMEM(sel_count.shape[::-1], jnp.int32),
            pltpu.SMEM(tile_radius.shape, jnp.int32),
            pltpu.VMEM((2,) + flat, BF16),
            pltpu.VMEM((2, heads, keys, depth), BF16),
            pltpu.VMEM((heads, 2, rows, depth), F32),
            pltpu.VMEM((heads, chips, 2, rows, depth), F32),
            pltpu.VMEM((heads, chips, 2, rows, depth), BF16),
            pltpu.VMEM((heads, chips, 2, rows, depth), BF16),
            pltpu.VMEM((heads, chips, 2, rows, depth), BF16),
            pltpu.VMEM((heads, chips, 2, rows, depth), BF16),
            pltpu.VMEM((heads, sides, 2, trows * tile, depth), BF16),
            pltpu.VMEM((heads, sides, 2, trows * tile, depth), BF16),
            dma((3,)), dma((2,)), dma((heads, 2)),
            dma((heads,)), dma((heads,)),
            dma((heads, chips, 2)), dma((heads, chips, 2)),
            dma((heads, chips, 2)), dma((heads, chips, 2)),
            dma((heads, sides, trows)), dma((heads, sides, trows)),
            dma((heads, chips, 2)), dma((heads, chips, 2)),
            dma((heads, chips, 2)), dma((heads, chips, 2)),
            dma((heads, sides)), dma((heads, sides)),
        ],
        compiler_params=pltpu.CompilerParams(
            collective_id=0, has_side_effects=True, vmem_limit_bytes=62 * 1024 * 1024),
        cost_estimate=pl.CostEstimate(
            flops=10 * heads * rows * keys * depth,
            bytes_accessed=14 * heads * rows * depth,
            transcendentals=heads * rows * keys),
    )(
        query_rows.reshape(flat), key_rows.reshape(flat), value_rows.reshape(flat),
        grad_out.reshape(flat), sel_tiles, sel_count.T, tile_radius,
    )
    results = pl.pallas_call(
        unstack,
        out_shape=(out, out, out),
        in_specs=[vmem],
        out_specs=(hbm,) * 3,
        scratch_shapes=[dma((3,))],
        compiler_params=pltpu.CompilerParams(vmem_limit_bytes=1024 * 1024),
    )(stacked)
    return tuple(r.reshape(query_rows.shape) for r in results)


def solution(mesh):
    block = P("hd", "hb", "wb", None, None)
    return jax.shard_map(
        functools.partial(on_device, mesh.shape["hb"], mesh.shape["wb"]),
        mesh=mesh,
        in_specs=(block, block, block, block, P(None, "wb", None), P(None, "wb"), P("hd")),
        out_specs=(block, block, block),
        check_vma=False,
    )
```

```python
import functools

import jax
import jax.numpy as jnp
from jax import lax
from jax.experimental import pallas as pl
from jax.experimental.pallas import tpu as pltpu
from jax.sharding import PartitionSpec as P

MESH = pl.DeviceIdType.MESH
F32 = jnp.float32
BF16 = jnp.bfloat16
NT = (((1,), (1,)), ((), ()))
NN = (((1,), (0,)), ((), ()))
TN = (((0,), (0,)), ((), ()))


def dot(a, b, dims):
    return lax.dot_general(a, b, dims, preferred_element_type=F32)


def kernel(
    dims,
    q_hbm, k_hbm, v_hbm, g_hbm, sel_hbm, count_hbm, radius_hbm,
    out_ref,
    sel_ref, count_ref, radius_ref, qg, kv, acc_own, acc_chip, tx_sib, rx_sib, tx_chip, rx_chip, tx_edge, rx_edge,
    i_sem, q_sem, kv_sem, s_kvsib, r_kvsib, s_kvchip, r_kvchip, s_relay, r_relay, s_kvedge, r_kvedge,
    s_psib, r_psib, s_pchip, r_pchip, s_pedge, r_pedge,
):
    heads, trows, tcols, tile, picks, n_hb, n_wb, factor = dims
    rows = trows * tcols * tile
    chips = n_hb // 2
    me = lax.axis_index("hb")
    w = lax.axis_index("wb")
    chip, core = me // 2, me % 2
    sib = chip * 2 + 1 - core
    near_rows = 2 * rows + min(2, n_wb - 1) * trows * tile
    to_chip = {j: ((chip + j) % chips) * 2 + core for j in range(1, chips)}
    from_chip = {j: ((chip + chips - j) % chips) * 2 + core for j in range(1, chips)}
    if n_wb == 1:
        links = []
    elif n_wb == 2:
        links = [(None, 1 - w, 0, 0, (1 - w) * (tcols - 1))]
    else:
        links = [(w > 0, w - 1, 0, 1, 0), (w < n_wb - 1, w + 1, 1, 0, tcols - 1)]

    def guarded(there, fn):
        if there is None:
            fn()
        else:
            pl.when(there)(fn)

    def remote(src, dst, send, recv, axis, to):
        return pltpu.make_async_remote_copy(
            src_ref=src, dst_ref=dst, send_sem=send, recv_sem=recv,
            device_id={axis: to}, device_id_type=MESH,
        )

    own_kv = []
    for h in range(heads):
        own_kv.append((
            pltpu.make_async_copy(k_hbm.at[h], kv.at[0, h, pl.ds(0, rows)], kv_sem.at[h, 0]),
            pltpu.make_async_copy(v_hbm.at[h], kv.at[1, h, pl.ds(0, rows)], kv_sem.at[h, 1]),
        ))
        for c in own_kv[-1]:
            c.start()
    own_q = [
        pltpu.make_async_copy(q_hbm, qg.at[0], q_sem.at[0]),
        pltpu.make_async_copy(g_hbm, qg.at[1], q_sem.at[1]),
    ]
    indices = [
        pltpu.make_async_copy(src, dst, i_sem.at[i])
        for i, (src, dst) in enumerate(
            ((sel_hbm, sel_ref), (count_hbm, count_ref), (radius_hbm, radius_ref)))
    ]
    for c in own_q + indices:
        c.start()

    barrier = pltpu.get_barrier_semaphore()
    pl.semaphore_signal(barrier, inc=1, device_id={"hb": sib}, device_id_type=MESH)
    for j in range(1, chips):
        pl.semaphore_signal(barrier, inc=1, device_id={"hb": to_chip[j]}, device_id_type=MESH)
    for there, peer, _, _, _ in links:
        def hello(peer=peer):
            pl.semaphore_signal(barrier, inc=1, device_id={"wb": peer}, device_id_type=MESH)
        guarded(there, hello)
    if n_wb > 2:
        for slot, (there, _, _, _, _) in enumerate(links):
            def blank(slot=slot):
                at = 2 * rows + slot * trows * tile
                kv[:, :, pl.ds(at, trows * tile), :] = jnp.zeros(
                    (2, heads, trows * tile, kv.shape[-1]), BF16)
            pl.when(jnp.logical_not(there))(blank)
    greeted = chips
    for there, _, _, _, _ in links:
        greeted = greeted + (1 if there is None else jnp.where(there, 1, 0))
    pl.semaphore_wait(barrier, greeted)

    def slot_at(s):
        return pl.ds(s * rows if s < 2 else near_rows + (s - 2) * rows, rows)

    def edge_at(slot, r):
        return pl.ds(2 * rows + (slot * trows + r) * tile, tile)

    def kv_chip(h, j, i):
        return remote((k_hbm, v_hbm)[i].at[h], kv.at[i, h, slot_at(2 * j)],
                      s_kvchip.at[h, j, i], r_kvchip.at[h, j, i], "hb", to_chip[j])

    def kv_sib(h):
        return remote(kv.at[:, h, slot_at(0)], kv.at[:, h, slot_at(1)],
                      s_kvsib.at[h], r_kvsib.at[h], "hb", sib)

    def relay(h, j, i):
        return remote(kv.at[i, h, slot_at(2 * j)], kv.at[i, h, slot_at(2 * j + 1)],
                      s_relay.at[h, j, i], r_relay.at[h, j, i], "hb", sib)

    def own_tile(r, col):
        return pl.ds(pl.multiple_of((r * tcols + col) * tile, tile), tile)

    def kv_edge(h, link, r, arriving=False):
        _, peer, here, away, col = link
        slot = here if arriving else away
        return remote(kv.at[:, h, own_tile(r, col)], kv.at[:, h, edge_at(slot, r)],
                      s_kvedge.at[h, away, r], r_kvedge.at[h, slot, r], "wb", peer)

    def p_sib(h, j, i):
        return remote(tx_sib.at[h, j, i], rx_sib.at[h, j, i],
                      s_psib.at[h, j, i], r_psib.at[h, j, i], "hb", sib)

    def p_chip(h, j, i):
        return remote(tx_chip.at[h, j, i], rx_chip.at[h, j, i],
                      s_pchip.at[h, j, i], r_pchip.at[h, j, i], "hb", from_chip[j])

    def p_edge(h, link, arriving=False):
        _, peer, here, away, _ = link
        slot = here if arriving else away
        return remote(tx_edge.at[h, here], rx_edge.at[h, slot],
                      s_pedge.at[h, here], r_pedge.at[h, slot], "wb", peer)

    def send_chip(h):
        for j in range(1, chips):
            for i in range(2):
                kv_chip(h, j, i).start()

    send_chip(0)
    for h in range(heads):
        for c in own_kv[h]:
            c.wait()
        kv_sib(h).start()
        for link in links:
            def send(link=link, h=h):
                for r in range(trows):
                    kv_edge(h, link, r).start()
            guarded(link[0], send)

    if heads > 1:
        send_chip(1)
    for c in indices:
        c.wait()
    lane_tile = lax.broadcasted_iota(jnp.int32, (1, rows), 1) // tile
    lane_row = me * trows + lane_tile // tcols
    lane_col = lane_tile % tcols
    chosen = []
    for s in range(picks):
        entry = jnp.full((1, rows), -1, jnp.int32)
        for r in range(trows):
            for c in range(tcols):
                row = me * trows + r
                value = jnp.where(s < count_ref[c, row], sel_ref[row, c, s], -1)
                entry = jnp.where(lane_tile == r * tcols + c, value, entry)
        chosen.append(entry)
    spread, picked = [], []
    for s in range(n_hb):
        j = s // 2
        group = ((chip + chips - j) % chips) * 2 + (core if s % 2 == 0 else 1 - core)
        for r in range(trows):
            for c in range(tcols):
                key_row = group * trows + r
                spread.append(jnp.abs(lane_row - key_row) + jnp.abs(lane_col - c))
                at = key_row * tcols + c
                hit = functools.reduce(jnp.logical_or, [e == at for e in chosen])
                picked.append(hit)
    beside = []
    for there, _, slot, _, col in links:
        for r in range(trows):
            near = lane_tile == r * tcols + col
            if there is not None:
                near = jnp.logical_and(near, there)
            beside.append(near)

    for c in own_q:
        c.wait()

    near_tiles = 2 * trows * tcols

    def product(i, h, at):
        return dot(kv[i, h, at], qg[i, h], NT)

    def near_products(h):
        kv_sib(h).wait_recv()
        for link in links:
            def arrive(link=link):
                for r in range(trows):
                    kv_edge(h, link, r, True).wait_recv()
            guarded(link[0], arrive)
        return [product(i, h, slice(0, near_rows)) for i in range(2)]

    def softmax(h, blocks):
        radius = radius_ref[h]
        bias = [jnp.where(jnp.logical_or(sp <= radius, pk), 0.0, -jnp.inf)
                for sp, pk in zip(spread, picked)]
        edge = [jnp.where(jnp.logical_and(near, radius >= 1), 0.0, -jnp.inf) for near in beside]
        bias = bias[:near_tiles] + edge + bias[near_tiles:]
        s_t, d_t = [], []
        for scores, slopes in blocks:
            for i in range(scores.shape[0] // tile):
                cut = slice(i * tile, (i + 1) * tile)
                s_t.append(scores[cut] * factor + bias[len(s_t)])
                d_t.append(slopes[cut])
        top = jnp.max(functools.reduce(jnp.maximum, s_t), axis=0, keepdims=True)
        e_t = [jnp.exp(s - top) for s in s_t]
        total = jnp.sum(functools.reduce(jnp.add, e_t), axis=0, keepdims=True)
        mixed = jnp.sum(functools.reduce(jnp.add, [e * d for e, d in zip(e_t, d_t)]),
                        axis=0, keepdims=True)
        inverse = 1.0 / total
        delta = mixed * inverse
        probs = [e * inverse for e in e_t]
        half = jnp.concatenate([p.astype(BF16) for p in probs], axis=0)
        grad = jnp.concatenate(
            [(p * ((d - delta) * factor)).astype(BF16) for p, d in zip(probs, d_t)], axis=0)
        return half, grad

    def pass_on(h):
        for i in range(2):
            for j in range(1, chips):
                kv_chip(h, j, i).wait_recv()
                relay(h, j, i).start()

    blocks = [near_products(0)]
    for h in range(2, heads):
        send_chip(h)
    pass_on(0)
    for h in range(heads):
        if chips > 1:
            far = []
            for i in range(2):
                for j in range(1, chips):
                    relay(h, j, i).wait_recv()
                far.append(product(i, h, slice(near_rows, near_rows + (n_hb - 2) * rows)))
            blocks.append(far)
        half, grad = softmax(h, blocks)
        q, g = qg[0, h], qg[1, h]
        if chips > 1:
            for i in (1, 0):
                part = dot((grad, half)[i][near_rows:], (q, g)[i], NN)
                for j in range(1, chips):
                    at = (2 * j - 2) * rows
                    tx_sib[h, j, i] = part[at + rows:at + 2 * rows].astype(BF16)
                    acc_chip[h, j, i] = part[at:at + rows]
                    p_sib(h, j, i).start()
        if h + 1 < heads:
            pass_on(h + 1)
        near_parts = (dot(grad[:near_rows], q, NN), dot(half[:near_rows], g, NN))
        for i, part in enumerate(near_parts):
            tx_sib[h, 0, i] = part[rows:2 * rows].astype(BF16)
            acc_own[h, i] = part[:rows]
            p_sib(h, 0, i).start()
        for link in links:
            at = 2 * rows + link[2] * trows * tile
            for i, part in enumerate(near_parts):
                tx_edge[h, link[2], i] = part[at:at + trows * tile].astype(BF16)
            guarded(link[0], lambda link=link, h=h: p_edge(h, link).start())
        out_ref[0, h] = dot(grad, kv[0, h], TN).astype(BF16)
        if h + 1 < heads:
            blocks = [near_products(h + 1)]
        for i in (1, 0):
            for j in range(1, chips):
                p_sib(h, j, i).wait_recv()
                tx_chip[h, j, i] = (acc_chip[h, j, i] + rx_sib[h, j, i].astype(F32)).astype(BF16)
                p_chip(h, j, i).start()

    for h in range(heads):
        for i in range(2):
            p_sib(h, 0, i).wait_recv()
        for link in links:
            there, _, here, _, col = link

            def add_edge(link=link, here=here, col=col, h=h):
                p_edge(h, link, True).wait_recv()
                for i in range(2):
                    for r in range(trows):
                        at = own_tile(r, col)
                        acc_own[h, i, at] += rx_edge[h, here, i, pl.ds(r * tile, tile)].astype(F32)
            guarded(there, add_edge)
        totals = [acc_own[h, i] + rx_sib[h, 0, i].astype(F32) for i in range(2)]
        for i in (1, 0):
            for j in range(1, chips):
                p_chip(h, j, i).wait_recv()
                totals[i] = totals[i] + rx_chip[h, j, i].astype(F32)
            out_ref[1 + i, h] = totals[i].astype(BF16)

    for h in range(heads):
        kv_sib(h).wait_send()
        for i in range(2):
            p_sib(h, 0, i).wait_send()
            for j in range(1, chips):
                for copy in (kv_chip, relay, p_sib, p_chip):
                    copy(h, j, i).wait_send()
        for link in links:
            def drain(link=link, h=h):
                for r in range(trows):
                    kv_edge(h, link, r).wait_send()
                p_edge(h, link).wait_send()
            guarded(link[0], drain)


def unstack(stacked, dq_hbm, dk_hbm, dv_hbm, sem):
    copies = [pltpu.make_async_copy(stacked.at[i], out, sem.at[i])
              for i, out in enumerate((dq_hbm, dk_hbm, dv_hbm))]
    for c in copies:
        c.start()
    for c in copies:
        c.wait()


def on_device(n_hb, n_wb, query_rows, key_rows, value_rows, grad_out, sel_tiles, sel_count, tile_radius):
    heads, trows, tcols, tile, depth = query_rows.shape
    picks = sel_tiles.shape[-1]
    rows = trows * tcols * tile
    chips = n_hb // 2
    sides = max(1, min(2, n_wb - 1))
    used = min(2, n_wb - 1)
    flat = (heads, rows, depth)
    keys = n_hb * rows + used * trows * tile
    dma = pltpu.SemaphoreType.DMA
    dims = (heads, trows, tcols, tile, picks, n_hb, n_wb, depth ** -0.5)
    hbm = pl.BlockSpec(memory_space=pltpu.HBM)
    vmem = pl.BlockSpec(memory_space=pltpu.VMEM)
    out = jax.ShapeDtypeStruct(flat, BF16)
    stacked = pl.pallas_call(
        functools.partial(kernel, dims),
        out_shape=pltpu.VMEM((3,) + flat, BF16),
        in_specs=[hbm] * 7,
        out_specs=vmem,
        scratch_shapes=[
            pltpu.SMEM(sel_tiles.shape, jnp.int32),
            pltpu.SMEM(sel_count.shape[::-1], jnp.int32),
            pltpu.SMEM(tile_radius.shape, jnp.int32),
            pltpu.VMEM((2,) + flat, BF16),
            pltpu.VMEM((2, heads, keys, depth), BF16),
            pltpu.VMEM((heads, 2, rows, depth), F32),
            pltpu.VMEM((heads, chips, 2, rows, depth), F32),
            pltpu.VMEM((heads, chips, 2, rows, depth), BF16),
            pltpu.VMEM((heads, chips, 2, rows, depth), BF16),
            pltpu.VMEM((heads, chips, 2, rows, depth), BF16),
            pltpu.VMEM((heads, chips, 2, rows, depth), BF16),
            pltpu.VMEM((heads, sides, 2, trows * tile, depth), BF16),
            pltpu.VMEM((heads, sides, 2, trows * tile, depth), BF16),
            dma((3,)), dma((2,)), dma((heads, 2)),
            dma((heads,)), dma((heads,)),
            dma((heads, chips, 2)), dma((heads, chips, 2)),
            dma((heads, chips, 2)), dma((heads, chips, 2)),
            dma((heads, sides, trows)), dma((heads, sides, trows)),
            dma((heads, chips, 2)), dma((heads, chips, 2)),
            dma((heads, chips, 2)), dma((heads, chips, 2)),
            dma((heads, sides)), dma((heads, sides)),
        ],
        compiler_params=pltpu.CompilerParams(
            collective_id=0, has_side_effects=True, vmem_limit_bytes=62 * 1024 * 1024),
        cost_estimate=pl.CostEstimate(
            flops=10 * heads * rows * keys * depth,
            bytes_accessed=14 * heads * rows * depth,
            transcendentals=heads * rows * keys),
    )(
        query_rows.reshape(flat), key_rows.reshape(flat), value_rows.reshape(flat),
        grad_out.reshape(flat), sel_tiles, sel_count.T, tile_radius,
    )
    results = pl.pallas_call(
        unstack,
        out_shape=(out, out, out),
        in_specs=[vmem],
        out_specs=(hbm,) * 3,
        scratch_shapes=[dma((3,))],
        compiler_params=pltpu.CompilerParams(vmem_limit_bytes=1024 * 1024),
    )(stacked)
    return tuple(r.reshape(query_rows.shape) for r in results)


def solution(mesh):
    block = P("hd", "hb", "wb", None, None)
    return jax.shard_map(
        functools.partial(on_device, mesh.shape["hb"], mesh.shape["wb"]),
        mesh=mesh,
        in_specs=(block, block, block, block, P(None, "wb", None), P(None, "wb"), P("hd")),
        out_specs=(block, block, block),
        check_vma=False,
    )
```
